256 devices in a mesh: sim: 32 (over z, y_lo, core), pen: 8 (over y_hi, x).
Axes of the slice: x: 4, y: 4 (y_hi: 2, y_lo: 2; y = y_hi * 2 + y_lo), z: 8, core: 2. Of those that a mesh axis runs over, the one named last changes fastest.
Arguments:
- density: float32 [1024, 32, 1024], P('sim', None, 'pen'), may hold values from 0.05 to 2
- velocity: float32 [3, 1024, 32, 1024], P(None, 'sim', None, 'pen'), may hold values from -4 to 4
- stencil_code: int32 [1024, 32, 1024], P('sim', None, 'pen'), may hold values from 0 to 7
- fractions: float32 [3, 1024, 32, 1024], P(None, 'sim', None, 'pen'), may hold values from 0 to 1
- targets: float32 [32, 32, 1024], P(None, 'sim', 'pen'), may hold values from 0.2 to 1.2
- view_start: int32 [32], replicated, may hold values from 0 to 1023
- view_sign: int32 [32], replicated, may hold values from 0 to 1
Outputs:
- density_new: float32 [1024, 32, 1024], P('sim', None, 'pen')
- velocity_new: float32 [3, 1024, 32, 1024], P(None, 'sim', None, 'pen')
- images: float32 [32, 32, 1024], P(None, 'sim', 'pen')
- density_grad: float32 [1024, 32, 1024], P('sim', None, 'pen')
The draws below stay inside these ranges and needn't reach their ends.
Inputs may be any that keep to these rules, and one draw needn't show every extreme that they name: `stencil_code`: bits 0, 1 and 2 of an entry belong to the first, second and third grid dimension.
All inputs are finite; a program needn't handle non-finite values.
Results may differ from the reference program's by a relative error of at most 0.0003.
Values sent between devices are 32-bit elements; how exact they have to be, the bound alone decides.
A program may use at most 192 MiB of HBM per device.

```python
import math
import jax
import jax.numpy as jnp
from jax import lax

NX = 1024
NY = 1024
VIEWS = 32
STEPS = 256
NZ = 32


def draw_velocity(key, part):
    key = jax.random.fold_in(key, 7)
    noise_part = 0.6 * jnp.clip(jax.random.normal(key, (3, NX, NZ, NY), jnp.float32), -4.0, 4.0)
    return noise_part


def with_ends(entries, rng, least, largest):
    spot = [jax.random.randint(jax.random.fold_in(rng, axis), (), 0, length) for axis, length in enumerate(entries.shape)]
    widest = entries.shape.index(max(entries.shape))
    next_to = spot[:widest] + [(spot[widest] + 1) % entries.shape[widest]] + spot[widest + 1:]
    return entries.at[tuple(spot)].set(least).at[tuple(next_to)].set(largest)


def block_levels(stream_key, extent, split, least, high):
    def one(dim, blocks):
        draws = jax.random.uniform(jax.random.fold_in(jax.random.fold_in(stream_key, 6), dim), (blocks,), jnp.float32, least / len(split), high / len(split))
        return jnp.repeat(jnp.exp(draws), extent[dim] // blocks).reshape((-1,) + (1,) * (len(extent) - dim - 1))

    level = one(*split[0])
    for cut in split[1:]:
        level = level * one(*cut)
    return level


def setup_inputs(seed: int = 0) -> dict:
    keys = jax.random.split(jax.random.key(seed), 8)
    return {
        "density": jnp.clip(0.05 + 1.95 * jax.random.uniform(keys[0], (NX, NZ, NY), jnp.float32) ** block_levels(keys[0], (NX, NZ, NY), ((0, 32), (2, 8)), -0.2, 0.2), 0.05, 2.0),
        "velocity": draw_velocity(jax.random.fold_in(keys[7], 71), 0),
        "stencil_code": with_ends(jax.random.randint(keys[2], (NX, NZ, NY), 0, 8), jax.random.fold_in(keys[2], 1), 0, 7).astype(jnp.int32),
        "fractions": jnp.clip(1.0 * jax.random.uniform(keys[3], (3, NX, NZ, NY), jnp.float32) ** block_levels(keys[3], (3, NX, NZ, NY), ((1, 32), (3, 8)), -0.2, 0.2), 0.0, 1.0),
        "targets": jnp.clip(0.2 + 1 * jax.random.uniform(keys[4], (VIEWS, NZ, NY), jnp.float32) ** block_levels(keys[4], (VIEWS, NZ, NY), ((1, 32), (2, 8)), -0.2, 0.2), 0.2, 1.2),
        "view_start": with_ends(jax.random.randint(keys[5], (VIEWS,), 0, NX), jax.random.fold_in(keys[5], 1), 0, NX - 1).astype(jnp.int32),
        "view_sign": with_ends(jax.random.randint(keys[6], (VIEWS,), 0, 2), jax.random.fold_in(keys[6], 1), 0, 1).astype(jnp.int32),
    }


shift_values = (-1, 0, 1)


def stencil_weights(offset_bit, fraction):
    lower_weight = jnp.where(offset_bit == 1, 1.0 - fraction, 0.0)
    center_weight = jnp.where(offset_bit == 1, fraction, 1.0 - fraction)
    upper_weight = jnp.where(offset_bit == 1, 0.0, fraction)
    return (lower_weight, center_weight, upper_weight)


def advect_field(values, weight_x, weight_z, weight_y):
    summed = jnp.zeros_like(values)
    for slot_x, shift_x in enumerate(shift_values):
        for slot_y, shift_y in enumerate(shift_values):
            shifted = jnp.roll(values, (-shift_x, -shift_y), axis=(0, 2))
            z_summed = jnp.zeros_like(values)
            for slot_z, shift_z in enumerate(shift_values):
                z_summed = z_summed + weight_z[slot_z] * jnp.roll(shifted, -shift_z, axis=1)
            summed = summed + weight_x[slot_x] * weight_y[slot_y] * z_summed
    return summed


def eigenvalue_axis(length):
    phases = jnp.arange(length, dtype=jnp.float32) * (math.pi / length)
    sines = jnp.sin(phases)
    return 4.0 * sines * sines


def reference(density, velocity, stencil_code, fractions, targets, view_start, view_sign):
    weight_x = stencil_weights(stencil_code % 2, fractions[0])
    weight_z = stencil_weights((stencil_code // 2) % 2, fractions[1])
    weight_y = stencil_weights((stencil_code // 4) % 2, fractions[2])
    density_new = advect_field(density, weight_x, weight_z, weight_y)
    advected = [advect_field(velocity[which], weight_x, weight_z, weight_y) for which in range(3)]
    divergence = (advected[0] - jnp.roll(advected[0], 1, axis=0)) + (advected[2] - jnp.roll(advected[2], 1, axis=2))
    eigenvalue = eigenvalue_axis(NX)[:, None, None] + eigenvalue_axis(NY)[None, None, :]
    at_anchor = (jnp.arange(NX)[:, None, None] == 0) & (jnp.arange(NY)[None, None, :] == 0)
    spectrum = jnp.fft.fft2(divergence, axes=(0, 2))
    solved = jnp.where(at_anchor, 0.0, spectrum / jnp.where(at_anchor, 1.0, -eigenvalue))
    pressure = jnp.real(jnp.fft.ifft2(solved, axes=(0, 2))).astype(jnp.float32)
    velocity_new = jnp.stack([
        advected[0] - (jnp.roll(pressure, -1, axis=0) - pressure),
        advected[1],
        advected[2] - (jnp.roll(pressure, -1, axis=2) - pressure),
    ])

    absorb = 2.0 / STEPS
    flat_density = density_new.reshape(NX, NZ * NY)
    offsets = jnp.arange(STEPS, dtype=jnp.int32)

    def one_view(gradient, inputs):
        view_first, view_flip, target = inputs
        cell_index = (view_first + (2 * view_flip - 1) * offsets) % NX
        samples = flat_density[cell_index]
        optical_depth = absorb * (jnp.cumsum(samples, axis=0) - samples)
        transmit = jnp.exp(-optical_depth)
        emitted = absorb * samples * transmit
        view_image = jnp.sum(emitted, axis=0)
        later_light = view_image[None, :] - jnp.cumsum(emitted, axis=0)
        residual = view_image - target.reshape(-1)
        grad_terms = STEPS * residual[None, :] * (absorb * transmit - absorb * later_light)
        gradient = gradient.at[cell_index].add(grad_terms)
        return gradient, view_image

    start_grad = jnp.zeros((NX, NZ * NY), jnp.float32)
    gradient, images = lax.scan(one_view, start_grad, (view_start, view_sign, targets))
    return density_new, velocity_new, images.reshape(VIEWS, NZ, NY), gradient.reshape(NX, NZ, NY)
```

```python
import functools

import jax
import jax.numpy as jnp
import numpy as np
from jax import lax
from jax.experimental import pallas as pl
from jax.experimental.pallas import tpu as pltpu
from jax.sharding import PartitionSpec as P

STEPS = 256
ABSORB = 2.0 / STEPS
LANES = 128
SEGMENTS = 8
MSG = 144
f32 = jnp.float32
bf16 = jnp.bfloat16


def hartley_pieces(length):
    index = np.arange(length)
    angles = (np.outer(index, index) % length) * (2.0 * np.pi / length)
    table = (np.cos(angles) + np.sin(angles)) / np.sqrt(length)
    pieces = []
    for _ in range(3):
        piece = table.astype(jnp.bfloat16)
        pieces.append(piece)
        table = table - piece.astype(np.float64)
    return np.stack(pieces)


def line_tables(length_y, length_x, local_x, layers):
    eig = 4.0 * np.sin(np.pi * np.arange(length_y) / length_y) ** 2
    half = eig / 2.0
    root = 1.0 / (1.0 + half + np.sqrt(half * (half + 2.0)))
    gap = 1.0 / root - root
    gap[0] = 1.0
    forward = -1.0 / gap
    backward = -1.0 / gap
    forward[0] = 1.0
    backward[0] = 0.0
    block = root**local_x
    closing = 1.0 - root**length_x
    closing[0] = 1.0
    closing = 1.0 / closing
    closing[0] = 0.0
    rows = np.stack([root, 1.0 / root, forward, backward, block, closing])
    rows = rows.reshape(6, length_y // LANES, 1, LANES)
    return np.repeat(rows, layers, axis=2).reshape(6, -1, LANES).astype(np.float32)


def split_two(values):
    high = values.astype(bf16)
    low = (values - high.astype(f32)).astype(bf16)
    return high, low


def split_three(values):
    high = values.astype(bf16)
    rest = values - high.astype(f32)
    mid = rest.astype(bf16)
    low = (rest - mid.astype(f32)).astype(bf16)
    return high, mid, low


def iota(shape, dim):
    return lax.broadcasted_iota(jnp.int32, shape, dim)


def matmul(a, b):
    return jnp.dot(a, b, preferred_element_type=f32)


def step_kernel(
    sizes,
    dens, vel, code, frac, targ, vstart, vsign, tables_hbm, lines,
    o_dens, o_vel, o_img, o_grad,
    ext, pack, xlo, xhi, pin, dens_k, ax_k, ay_k,
    rays, d_send, d_in, x_pieces, q_tab, spec, spec_end,
    c_send, c_in, c_out, c_ret, p_spec, y_pieces, o_send, o_in,
    prefix, w_light, v_light, gathered, rhs, sums, g_send, g_in,
    halo_s, halo_r, dens_s, dens_r, d_s, d_r, c_s, c_r, b_s, b_r, o_s, o_r, g_s, g_r, tab_sem,
):
    S, N, LX, K, VIEWS = sizes
    KP = K // N
    NX, NY = S * LX, N * LANES
    ROWS = KP * LX
    SEG = NX // SEGMENTS
    me = lax.axis_index("sim")
    pe = lax.axis_index("pen")

    def simp(off):
        return lax.rem(me + off + S, S)

    def penp(off):
        return lax.rem(pe + off + N, N)

    table_copies = [pltpu.make_async_copy(tables_hbm.at[t], q_tab.at[t], tab_sem.at[t]) for t in range(3)]
    for copy in table_copies:
        copy.start()

    barrier = pltpu.get_barrier_semaphore()

    def greet_sim(off, _):
        pl.semaphore_signal(barrier, inc=1, device_id={"sim": simp(off), "pen": pe}, device_id_type=pl.DeviceIdType.MESH)
        return 0

    def greet_pen(off, _):
        pl.semaphore_signal(barrier, inc=1, device_id={"sim": me, "pen": penp(off)}, device_id_type=pl.DeviceIdType.MESH)
        return 0

    lax.fori_loop(1, S, greet_sim, 0)
    lax.fori_loop(1, N, greet_pen, 0)
    corners = ((-1, -1), (-1, 1), (1, -1), (1, 1))
    for dx, dy in corners:
        pl.semaphore_signal(barrier, inc=1, device_id={"sim": simp(dx), "pen": penp(dy)}, device_id_type=pl.DeviceIdType.MESH)

    lane = iota((K, LANES), 1)

    def source(field, x):
        return dens[x] if field == 0 else vel[field - 1, x]

    def pack_body(x, carry):
        first, last = carry
        for field in range(4):
            cells = source(field, x)
            spot = field * LX + x
            here = lane == spot
            first = jnp.where(here, pltpu.roll(cells, spot, 1), first)
            last = jnp.where(here, pltpu.roll(cells, lax.rem(spot + 1, LANES), 1), last)
        return first, last

    nothing = jnp.zeros((K, LANES), f32)
    first, last = lax.fori_loop(0, LX, pack_body, (nothing, nothing))
    pack[0] = first
    pack[1] = last
    for field in range(4):
        pack[2 + field] = source(field, 0)
        pack[6 + field] = source(field, LX - 1)

    pl.semaphore_wait(barrier, (S - 1) + (N - 1) + 4)

    def remote(src, dst, s_sem, r_sem, sim, pen):
        return pltpu.make_async_remote_copy(
            src_ref=src, dst_ref=dst, send_sem=s_sem, recv_sem=r_sem,
            device_id={"sim": sim, "pen": pen}, device_id_type=pl.DeviceIdType.MESH,
        )

    halo = [
        remote(pack.at[pl.ds(6, 4)], xlo, halo_s.at[0], halo_r.at[0], simp(1), pe),
        remote(pack.at[pl.ds(2, 4)], xhi, halo_s.at[1], halo_r.at[1], simp(-1), pe),
    ]
    for side in range(2):
        for dx in (-1, 0, 1):
            slot = side * 3 + 1 + dx
            halo.append(
                remote(
                    pack.at[1 - side], pin.at[slot], halo_s.at[2 + slot], halo_r.at[2 + slot],
                    simp(-dx), penp(1 if side == 0 else -1),
                )
            )
    for copy in halo:
        copy.start()

    def spread_body(x, _):
        for field in range(4):
            cells = source(field, x)
            ext[0, field, x + 1] = pltpu.roll(cells, 1, 1)
            ext[1, field, x + 1] = cells
            ext[2, field, x + 1] = pltpu.roll(cells, LANES - 1, 1)
        return 0

    lax.fori_loop(0, LX, spread_body, 0)
    for copy in halo:
        copy.wait()

    is_first = lane == 0
    is_last = lane == LANES - 1

    def fix_body(x, _):
        for field in range(4):
            spot = field * LX + x
            left = pltpu.roll(pin[1], LANES - spot, 1)
            right = pltpu.roll(pin[4], LANES - 1 - spot, 1)
            ext[0, field, x + 1] = jnp.where(is_first, left, ext[0, field, x + 1])
            ext[2, field, x + 1] = jnp.where(is_last, right, ext[2, field, x + 1])
        return 0

    lax.fori_loop(0, LX, fix_body, 0)
    for row, rows, slot, at in ((0, xlo, 0, LX - 1), (LX + 1, xhi, 2, 0)):
        for field in range(4):
            spot = field * LX + at
            cells = rows[field]
            left = pltpu.roll(pin[slot], (LANES - spot) % LANES, 1)
            right = pltpu.roll(pin[3 + slot], LANES - 1 - spot, 1)
            ext[0, field, row] = jnp.where(is_first, left, pltpu.roll(cells, 1, 1))
            ext[1, field, row] = cells
            ext[2, field, row] = jnp.where(is_last, right, pltpu.roll(cells, LANES - 1, 1))

    def weights(bit, fraction):
        rest = 1.0 - fraction
        on = bit == 1
        return (jnp.where(on, rest, 0.0), jnp.where(on, fraction, rest), jnp.where(on, 0.0, fraction))

    def advect_body(x, _):
        codes = code[x]
        wx = weights(codes & 1, frac[0, x])
        wz = weights((codes >> 1) & 1, frac[1, x])
        wy = weights((codes >> 2) & 1, frac[2, x])
        totals = [None] * 4
        for slot, shift in ((1, 0), (0, -1), (2, 1)):
            if shift == 0:
                rx, ry = wx, wy
            else:
                amount = shift % K
                rx = [pltpu.roll(w, amount, 0) for w in wx]
                ry = [pltpu.roll(w, amount, 0) for w in wy]
            for field in range(4):
                term = None
                for sy in range(3):
                    part = (
                        rx[0] * ext[sy, field, x]
                        + rx[1] * ext[sy, field, x + 1]
                        + rx[2] * ext[sy, field, x + 2]
                    )
                    term = ry[sy] * part if term is None else term + ry[sy] * part
                if shift != 0:
                    term = pltpu.roll(term, (-shift) % K, 0)
                term = wz[slot] * term
                totals[field] = term if totals[field] is None else totals[field] + term
        o_dens[pl.ds(pl.multiple_of(x * K, 8), K), :] = totals[0]
        o_vel[pl.ds(pl.multiple_of(LX * K + x * K, 8), K), :] = totals[2]
        dens_k[pl.ds(x, K, stride=LX), :] = totals[0]
        ax_k[pl.ds(x, K, stride=LX), :] = totals[1]
        ay_k[pl.ds(x, K, stride=LX), :] = totals[3]
        return 0

    lax.fori_loop(0, LX, advect_body, 0)

    def sim_exchange(src, src_rows, dst, s_sem, r_sem):
        def descriptor(peer, start_at):
            a = src.at[pl.ds(pl.multiple_of(peer * src_rows, 8), src_rows)]
            b = dst.at[pl.ds(pl.multiple_of(start_at * src_rows, 8), src_rows)]
            return remote(a, b, s_sem.at[peer], r_sem.at[start_at], peer, pe)

        def start():
            def body(off, _):
                descriptor(simp(off), me).start()
                return 0

            lax.fori_loop(1, S, body, 0)

        def wait_recv():
            def body(off, _):
                peer = simp(off)
                descriptor(peer, peer).wait_recv()
                return 0

            lax.fori_loop(1, S, body, 0)

        def wait_send():
            def body(off, _):
                descriptor(simp(off), me).wait_send()
                return 0

            lax.fori_loop(1, S, body, 0)

        return start, wait_recv, wait_send

    def pen_exchange(src, dst, s_sem, r_sem):
        def descriptor(peer, start_at):
            return remote(src.at[peer], dst.at[start_at], s_sem.at[peer], r_sem.at[start_at], me, peer)

        def loop(method, swap):
            def body(off, _):
                peer = penp(off)
                getattr(descriptor(peer, peer if swap else pe), method)()
                return 0

            lax.fori_loop(1, N, body, 0)

        return (lambda: loop("start", False)), (lambda: loop("wait_recv", True)), (lambda: loop("wait_send", False))

    dens_x = sim_exchange(dens_k, LX, rays, dens_s, dens_r)
    dens_x[0]()
    mine = pl.ds(pl.multiple_of(me * LX, 8), LX)
    rays[mine, :] = dens_k[mine, :]

    sub_x = iota((LX, LANES), 0)
    lane_x = iota((LX, LANES), 1)

    def div_body(part, _):
        base = part * ROWS
        ends = []
        for layer in range(KP):
            at = pl.ds(pl.multiple_of(base + layer * LX, 8), LX)
            ax = ax_k[at, :]
            ay = ay_k[at, :]
            before_x = jnp.where(sub_x == 0, 0.0, pltpu.roll(ax, 1, 0))
            before_y = jnp.where(lane_x == 0, 0.0, pltpu.roll(ay, 1, 1))
            d_send[part, layer * LX : (layer + 1) * LX, :] = (ax - before_x) + (ay - before_y)
            ends.append(-ax[LX - 1 : LX, :])
        d_send[part, ROWS : ROWS + 8, :] = jnp.concatenate(ends + [jnp.zeros((8 - KP, LANES), f32)], axis=0)
        turned = jnp.transpose(ay_k[pl.ds(pl.multiple_of(base, 8), ROWS), :])
        d_send[part, ROWS + 8 : ROWS + 16, :] = jnp.broadcast_to(turned[LANES - 1 : LANES, :], (8, ROWS))
        return 0

    lax.fori_loop(0, N, div_body, 0)
    d_x = pen_exchange(d_send, d_in, d_s, d_r)
    d_x[0]()
    d_in[pe] = d_send[pe]
    for copy in table_copies:
        copy.wait()
    d_x[1]()

    lane_r = iota((ROWS, LANES), 1)
    for part in range(N):
        cells = d_in[part, 0:ROWS, :]
        row = d_in[(part - 1) % N, ROWS + 8 : ROWS + 9, :]
        column = jnp.transpose(jnp.broadcast_to(row, (LANES, ROWS)))
        cells = cells - jnp.where(lane_r == 0, column, 0.0)
        at = slice(part * LANES, (part + 1) * LANES)
        high, low = split_two(cells)
        x_pieces[0, 0:ROWS, at] = high
        x_pieces[1, 0:ROWS, at] = low
        high, low = split_two(d_in[part, ROWS:MSG, :])
        x_pieces[0, ROWS:MSG, at] = high
        x_pieces[1, ROWS:MSG, at] = low

    wide = 2 * LANES

    def forward_body(n, _):
        at = pl.ds(pl.multiple_of(n * wide, wide), wide)
        q0, q1 = q_tab[0, :, at], q_tab[1, :, at]
        result = matmul(x_pieces[0], q0) + (matmul(x_pieces[0], q1) + matmul(x_pieces[1], q0))
        for half in range(2):
            columns = result[:, half * LANES : (half + 1) * LANES]
            spec[pl.ds(pl.multiple_of((2 * n + half) * ROWS, 8), ROWS), :] = columns[0:ROWS]
            spec_end[2 * n + half] = columns[ROWS : ROWS + 8]
        return 0

    lax.fori_loop(0, NY // wide, forward_body, 0)

    LINES = N * KP
    root = lines[0]
    root_inv = lines[1]
    beyond = jnp.concatenate([spec_end[part, 0:KP, :] for part in range(N)], axis=0)
    flat = jnp.zeros((LINES, LANES), f32)

    def at_x(x):
        return pl.ds(x, LINES, stride=LX)

    def ends_body(i, carry):
        fwd, bwd, acc = carry
        fwd = spec[at_x(i), :] + root * fwd
        acc = acc + fwd
        bwd = root * (spec[at_x(LX - 1 - i), :] + bwd)
        return fwd, bwd, acc

    fwd, bwd, acc = lax.fori_loop(0, LX, ends_body, (flat, root * beyond, flat), unroll=2)
    fwd = fwd + root_inv * beyond

    def carry_row(row):
        return pl.ds(row, LINES, stride=8)

    c_send[carry_row(0), :] = fwd
    c_send[carry_row(1), :] = bwd
    c_send[carry_row(2), :] = acc
    for row in range(3, 8):
        c_send[carry_row(row), :] = flat
    c_x = sim_exchange(c_send, 8, c_in, c_s, c_r)
    c_x[0]()
    my_carry = pl.ds(pl.multiple_of(me * 8, 8), 8)
    c_in[my_carry, :] = c_send[my_carry, :]

    dens_x[1]()

    def strided(x):
        return pl.ds(x, SEGMENTS, stride=SEG)

    def chain(x):
        return pl.ds(pl.multiple_of(x * SEGMENTS, SEGMENTS), SEGMENTS)

    seg0 = jnp.zeros((SEGMENTS, LANES), f32)

    def scan_body(i, carry):
        depth, down, up = carry
        back = SEG - 1 - i
        glow = ABSORB * rays[strided(i), :]
        prefix[chain(i), :] = depth
        depth = depth + glow
        down = glow + jnp.exp(-glow) * down
        v_light[chain(i), :] = down
        glow_b = ABSORB * rays[strided(back), :]
        up = glow_b + jnp.exp(-glow_b) * up
        w_light[chain(back), :] = up
        return depth, down, up

    seg_depth, seg_down, seg_up = lax.fori_loop(0, SEG, scan_body, (seg0, seg0, seg0), unroll=4)
    seg_pass = jnp.exp(-seg_depth)
    one = jnp.zeros((1, LANES), f32)
    total_depth, run_down, run_up = one, one, one
    starts = []
    for g in range(SEGMENTS):
        starts.append(total_depth)
        total_depth = total_depth + seg_depth[g : g + 1, :]
        run_down = seg_down[g : g + 1, :] + seg_pass[g : g + 1, :] * run_down
        h = SEGMENTS - 1 - g
        run_up = seg_up[h : h + 1, :] + seg_pass[h : h + 1, :] * run_up
    total_pass = jnp.exp(-total_depth)
    closing = 1.0 / (1.0 - total_pass)
    run_down = run_down * closing
    run_up = run_up * closing
    downs, ups = [], []
    for g in range(SEGMENTS):
        downs.append(run_down)
        run_down = seg_down[g : g + 1, :] + seg_pass[g : g + 1, :] * run_down
        h = SEGMENTS - 1 - g
        ups.append(run_up)
        run_up = seg_up[h : h + 1, :] + seg_pass[h : h + 1, :] * run_up
    start_depth = jnp.concatenate(starts, axis=0)
    down_in = jnp.concatenate(downs, axis=0)
    up_in = jnp.concatenate(ups[::-1], axis=0)

    def finish_body(i, _):
        glow = ABSORB * rays[strided(i), :]
        depth = prefix[chain(i), :]
        v_light[chain(i), :] = v_light[chain(i), :] + jnp.exp(-(depth + glow)) * down_in
        w_light[chain(i), :] = w_light[chain(i), :] + jnp.exp(depth - seg_depth) * up_in
        prefix[chain(i), :] = depth + start_depth
        return 0

    lax.fori_loop(0, SEG, finish_body, 0, unroll=4)

    c_x[1]()
    block = lines[4, pl.ds(me, 1), :]
    close = lines[5, pl.ds(me, 1), :]
    lone = jnp.logical_and(iota((1, LANES), 1) == 0, me < KP)

    def carry_at(i, row):
        return pl.ds(8 * i + row, 1)

    def around_body(i, carry):
        a, b = carry
        a = c_in[carry_at(i, 0), :] + block * a
        b = c_in[carry_at(S - 1 - i, 1), :] + block * b
        return a, b

    a, b = lax.fori_loop(0, S, around_body, (one, one))

    def carry_body(i, carry):
        a, b, total = carry
        j = S - 1 - i
        c_out[carry_at(i, 0), :] = a
        c_out[carry_at(j, 1), :] = b
        total = total + (c_in[carry_at(i, 2), :] + LX * a)
        return c_in[carry_at(i, 0), :] + block * a, c_in[carry_at(j, 1), :] + block * b, total

    _, _, total = lax.fori_loop(0, S, carry_body, (a * close, b * close, one))
    mean = total * (1.0 / NX)

    def lone_body(i, offset):
        slope = c_out[carry_at(i, 0), :] - mean
        c_out[carry_at(i, 0), :] = jnp.where(lone, slope, c_out[carry_at(i, 0), :])
        c_out[carry_at(i, 1), :] = jnp.where(lone, offset, c_out[carry_at(i, 1), :])
        return offset + (c_in[carry_at(i, 2), :] + LX * slope)

    lax.fori_loop(0, S, lone_body, one)
    for row in range(2, 8):
        c_out[carry_row(row), :] = flat
    b_x = sim_exchange(c_out, 8, c_ret, b_s, b_r)
    b_x[0]()
    c_ret[my_carry, :] = c_out[my_carry, :]

    sub_v = iota((VIEWS, LANES), 0)
    lane_m = iota((1, 6 * VIEWS), 1)
    view_m = lax.rem(lane_m, VIEWS)

    def where_is(x):
        return lax.rem(x, SEG) * SEGMENTS + lax.div(x, SEG)

    def view_body(v, carry):
        ups_v, start_m, up_m = carry
        x0 = vstart[v]
        up = vsign[v] == 1
        far = jnp.where(up, x0 + STEPS, x0 - STEPS)
        wraps = jnp.logical_or(far >= NX, far < 0)
        xe = jnp.where(far >= NX, far - NX, jnp.where(far < 0, far + NX, far))
        out = []
        for x in (x0, xe):
            at = pl.ds(where_is(x), 1)
            depth = prefix[at, :]
            depth = jnp.where(up, depth, -(depth + ABSORB * rays[pl.ds(x, 1), :]))
            out.append((depth, jnp.where(up, w_light[at, :], v_light[at, :])))
        gathered[0, pl.ds(v, 1), :] = out[0][0]
        gathered[1, pl.ds(v, 1), :] = out[0][1]
        gathered[2, pl.ds(v, 1), :] = out[1][0] + jnp.where(wraps, total_depth, 0.0)
        gathered[3, pl.ds(v, 1), :] = out[1][1]
        flag = vsign[v]
        return (
            jnp.where(sub_v == v, flag, ups_v),
            jnp.where(view_m == v, x0, start_m),
            jnp.where(view_m == v, flag, up_m),
        )

    none_m = jnp.zeros((1, 6 * VIEWS), jnp.int32)
    ups_v, start_m, up_m = lax.fori_loop(0, VIEWS, view_body, (jnp.zeros((VIEWS, LANES), jnp.int32), none_m, none_m))
    entry, light0, leave, light1 = gathered[0], gathered[1], gathered[2], gathered[3]
    seen_through = jnp.exp(entry - leave) * light1
    picture = light0 - seen_through
    o_img[:, 0, :] = picture
    pull = (STEPS * ABSORB) * (picture - targ[:, 0, :])
    coef = pull * jnp.exp(entry)
    alpha = jnp.where(ups_v == 1, coef, 0.0)
    gamma = jnp.where(ups_v == 1, 0.0, coef)
    beta = pull * seen_through
    for slot, value in enumerate((alpha, gamma, beta)):
        wrapped = beta if slot == 2 else value * total_pass
        both = jnp.concatenate([value, wrapped], axis=0)
        for t, piece in enumerate(split_three(both)):
            rhs[t * 2 * VIEWS : (t + 1) * 2 * VIEWS, slot * LANES : (slot + 1) * LANES] = piece

    kind = lax.rem(lax.div(lane_m, VIEWS), 2) == 1
    tile = 256

    def window_body(n, _):
        row = n * tile + iota((tile, 6 * VIEWS), 0)
        x = lax.rem(row, SEGMENTS) * SEG + lax.div(row, SEGMENTS)
        delta = jnp.where(up_m == 1, x - start_m, start_m - x)
        back = delta < 0
        inside = jnp.where(back, delta + NX, delta) < STEPS
        chosen = jnp.logical_and(inside, jnp.logical_xor(back, jnp.logical_not(kind)))
        mask = jnp.where(chosen, 1.0, 0.0).astype(bf16)
        sums[pl.ds(pl.multiple_of(n * tile, tile), tile), :] = matmul(mask, rhs[...])
        return 0

    lax.fori_loop(0, NX // tile, window_body, 0)

    def grad_body(i, _):
        glow = ABSORB * rays[strided(i), :]
        depth = prefix[chain(i), :]
        terms = sums[chain(i), :]
        g_send[strided(i), :] = (
            jnp.exp(-depth) * (1.0 - w_light[chain(i), :] + glow) * terms[:, 0:LANES]
            + jnp.exp(depth + glow) * (1.0 - v_light[chain(i), :] + glow) * terms[:, LANES : 2 * LANES]
            + terms[:, 2 * LANES : 3 * LANES]
        )
        return 0

    lax.fori_loop(0, SEG, grad_body, 0, unroll=4)
    g_x = sim_exchange(g_send, LX, g_in, g_s, g_r)
    g_x[0]()
    g_in[mine, :] = g_send[mine, :]

    b_x[1]()
    factor_f = lines[2]
    factor_b = lines[3]
    alone = jnp.logical_and(iota((LINES, LANES), 1) == 0, iota((LINES, LANES), 0) < KP)
    first_f = c_ret[carry_row(0), :]
    tail = c_ret[carry_row(1), :]
    back_in = tail + root * beyond

    def back_body(i, bwd):
        x = LX - 1 - i
        p_spec[at_x(x), :] = factor_b * bwd
        return root * (spec[at_x(x), :] + bwd)

    lax.fori_loop(0, LX, back_body, back_in, unroll=2)

    def front_body(x, carry):
        fwd, height = carry
        fwd = spec[at_x(x), :] + root * fwd
        p_spec[at_x(x), :] = p_spec[at_x(x), :] + factor_f * jnp.where(alone, height, fwd)
        return fwd, height + fwd

    fwd, height = lax.fori_loop(0, LX, front_body, (first_f, tail), unroll=2)
    after = factor_f * jnp.where(alone, height, root * fwd) + factor_b * (root_inv * back_in)
    for part in range(N):
        at = slice(part * LANES, (part + 1) * LANES)
        for t, piece in enumerate(split_three(p_spec[part * ROWS : (part + 1) * ROWS, :])):
            y_pieces[t, 0:ROWS, at] = piece
        end = jnp.concatenate([after[part * KP : (part + 1) * KP], jnp.zeros((MSG - ROWS - KP, LANES), f32)], axis=0)
        for t, piece in enumerate(split_three(end)):
            y_pieces[t, ROWS:MSG, at] = piece

    def inverse_body(n, _):
        at = pl.ds(pl.multiple_of(n * wide, wide), wide)
        q0, q1, q2 = q_tab[0, :, at], q_tab[1, :, at], q_tab[2, :, at]
        y0, y1, y2 = y_pieces[0], y_pieces[1], y_pieces[2]
        small = matmul(y1, q1) + matmul(y0, q2) + matmul(y2, q0)
        result = matmul(y0, q0) + (matmul(y1, q0) + matmul(y0, q1) + small)
        o_send[2 * n, :, :] = result[:, 0:LANES]
        o_send[2 * n + 1, :, :] = result[:, LANES:wide]
        return 0

    lax.fori_loop(0, NY // wide, inverse_body, 0)
    for part in range(N):
        turned = jnp.transpose(o_send[(part + 1) % N, 0:ROWS, :])
        o_send[part, ROWS + 8 : ROWS + 16, :] = jnp.broadcast_to(turned[0:1, :], (8, ROWS))
    o_x = pen_exchange(o_send, o_in, o_s, o_r)
    o_x[0]()
    o_in[pe] = o_send[pe]
    o_x[1]()

    def velocity_body(part, _):
        column = jnp.transpose(jnp.broadcast_to(o_in[part, ROWS + 8 : ROWS + 9, :], (LANES, ROWS)))
        for layer in range(KP):
            k = part * KP + layer
            at = pl.ds(pl.multiple_of(k * LX, 8), LX)
            here = o_in[part, layer * LX : (layer + 1) * LX, :]
            above = o_in[part, ROWS + layer : ROWS + layer + 1, :]
            next_x = jnp.where(sub_x == LX - 1, above, pltpu.roll(here, LX - 1, 0))
            next_y = jnp.where(
                lane_x == LANES - 1, column[layer * LX : (layer + 1) * LX, :], pltpu.roll(here, LANES - 1, 1)
            )
            o_vel[pl.ds(k, LX, stride=K), :] = ax_k[at, :] - (next_x - here)
            o_vel[pl.ds(2 * LX * K + k, LX, stride=K), :] = ay_k[at, :] - (next_y - here)
        return 0

    lax.fori_loop(0, N, velocity_body, 0)

    g_x[1]()

    def back_home(k, _):
        o_grad[pl.ds(k, LX, stride=K), :] = g_in[pl.ds(pl.multiple_of(k * LX, 8), LX), :]
        return 0

    lax.fori_loop(0, K, back_home, 0)
    for copy_sends in (dens_x[2], d_x[2], c_x[2], b_x[2], g_x[2], o_x[2]):
        copy_sends()


def solution(mesh):
    S, N = mesh.shape["sim"], mesh.shape["pen"]

    def shards(density, velocity, stencil_code, fractions, targets, view_start, view_sign):
        LX, K, LY = density.shape
        VIEWS = targets.shape[0]
        NX, NY = LX * S, LY * N
        tables = jnp.asarray(hartley_pieces(NY))
        lines = jnp.asarray(line_tables(NY, NX, LX, K // N))
        vmem = pl.BlockSpec(memory_space=pltpu.VMEM)
        smem = pl.BlockSpec(memory_space=pltpu.SMEM)
        dma = pltpu.SemaphoreType.DMA
        scratch = [
            pltpu.VMEM((3, 4, LX + 2, K, LY), f32),
            pltpu.VMEM((10, K, LY), f32),
            pltpu.VMEM((4, K, LY), f32),
            pltpu.VMEM((4, K, LY), f32),
            pltpu.VMEM((6, K, LY), f32),
            pltpu.VMEM((K * LX, LY), f32),
            pltpu.VMEM((K * LX, LY), f32),
            pltpu.VMEM((K * LX, LY), f32),
            pltpu.VMEM((NX, LY), f32),
            pltpu.VMEM((N, MSG, LY), f32),
            pltpu.VMEM((N, MSG, LY), f32),
            pltpu.VMEM((2, MSG, NY), bf16),
            pltpu.VMEM((3, NY, NY), bf16),
            pltpu.VMEM((N * 128, LANES), f32),
            pltpu.VMEM((N, 8, LANES), f32),
            pltpu.VMEM((S * 8, LANES), f32),
            pltpu.VMEM((S * 8, LANES), f32),
            pltpu.VMEM((S * 8, LANES), f32),
            pltpu.VMEM((S * 8, LANES), f32),
            pltpu.VMEM((N * 128, LANES), f32),
            pltpu.VMEM((3, MSG, NY), bf16),
            pltpu.VMEM((N, MSG, LY), f32),
            pltpu.VMEM((N, MSG, LY), f32),
            pltpu.VMEM((NX, LY), f32),
            pltpu.VMEM((NX, LY), f32),
            pltpu.VMEM((NX, LY), f32),
            pltpu.VMEM((4, VIEWS, LY), f32),
            pltpu.VMEM((6 * VIEWS, 3 * LY), bf16),
            pltpu.VMEM((NX, 3 * LY), f32),
            pltpu.VMEM((NX, LY), f32),
            pltpu.VMEM((K * LX, LY), f32),
            dma((8,)), dma((8,)),
            dma((S,)), dma((S,)),
            dma((N,)), dma((N,)),
            dma((S,)), dma((S,)),
            dma((S,)), dma((S,)),
            dma((N,)), dma((N,)),
            dma((S,)), dma((S,)),
            dma((3,)),
        ]
        density_new, velocity_new, images, gradient = pl.pallas_call(
            functools.partial(step_kernel, (S, N, LX, K, VIEWS)),
            out_shape=(
                jax.ShapeDtypeStruct((LX * K, LY), f32),
                jax.ShapeDtypeStruct((3 * LX * K, LY), f32),
                jax.ShapeDtypeStruct(targets.shape, f32),
                jax.ShapeDtypeStruct((LX * K, LY), f32),
            ),
            in_specs=[vmem, vmem, vmem, vmem, vmem, smem, smem, pl.BlockSpec(memory_space=pl.ANY), vmem],
            out_specs=(vmem, vmem, vmem, vmem),
            scratch_shapes=scratch,
            compiler_params=pltpu.CompilerParams(
                collective_id=0, has_side_effects=True, vmem_limit_bytes=60 * 1024 * 1024
            ),
        )(density, velocity, stencil_code, fractions, targets, view_start, view_sign, tables, lines)
        return (
            density_new.reshape(LX, K, LY),
            velocity_new.reshape(3, LX, K, LY),
            images,
            gradient.reshape(LX, K, LY),
        )

    return jax.shard_map(
        shards,
        mesh=mesh,
        in_specs=(
            P("sim", None, "pen"),
            P(None, "sim", None, "pen"),
            P("sim", None, "pen"),
            P(None, "sim", None, "pen"),
            P(None, "sim", "pen"),
            P(),
            P(),
        ),
        out_specs=(
            P("sim", None, "pen"),
            P(None, "sim", None, "pen"),
            P(None, "sim", "pen"),
            P("sim", None, "pen"),
        ),
        check_vma=False,
    )
```

```python
import functools

import jax
import jax.numpy as jnp
import numpy as np
from jax import lax
from jax.experimental import pallas as pl
from jax.experimental.pallas import tpu as pltpu
from jax.sharding import PartitionSpec as P

STEPS = 256
ABSORB = 2.0 / STEPS
LANES = 128
SEGMENTS = 8
MSG = 144
f32 = jnp.float32
bf16 = jnp.bfloat16


def hartley_pieces(length):
    index = np.arange(length)
    angles = (np.outer(index, index) % length) * (2.0 * np.pi / length)
    table = (np.cos(angles) + np.sin(angles)) / np.sqrt(length)
    pieces = []
    for _ in range(3):
        piece = table.astype(jnp.bfloat16)
        pieces.append(piece)
        table = table - piece.astype(np.float64)
    return np.stack(pieces)


def line_tables(length_y, length_x, local_x, layers):
    eig = 4.0 * np.sin(np.pi * np.arange(length_y) / length_y) ** 2
    half = eig / 2.0
    root = 1.0 / (1.0 + half + np.sqrt(half * (half + 2.0)))
    gap = 1.0 / root - root
    gap[0] = 1.0
    forward = -1.0 / gap
    backward = -1.0 / gap
    forward[0] = 1.0
    backward[0] = 0.0
    block = root**local_x
    closing = 1.0 - root**length_x
    closing[0] = 1.0
    closing = 1.0 / closing
    closing[0] = 0.0
    rows = np.stack([root, 1.0 / root, forward, backward, block, closing])
    rows = rows.reshape(6, length_y // LANES, 1, LANES)
    return np.repeat(rows, layers, axis=2).reshape(6, -1, LANES).astype(np.float32)


def split_two(values):
    high = values.astype(bf16)
    low = (values - high.astype(f32)).astype(bf16)
    return high, low


def split_three(values):
    high = values.astype(bf16)
    rest = values - high.astype(f32)
    mid = rest.astype(bf16)
    low = (rest - mid.astype(f32)).astype(bf16)
    return high, mid, low


def iota(shape, dim):
    return lax.broadcasted_iota(jnp.int32, shape, dim)


def matmul(a, b):
    return jnp.dot(a, b, preferred_element_type=f32)


def step_kernel(
    sizes,
    dens, vel, code, frac, targ, vstart, vsign, tables_hbm, lines,
    o_dens, o_vel, o_img, o_grad,
    ext, pack, xlo, xhi, pin, dens_k, ax_k, ay_k,
    rays, d_send, d_in, x_pieces, q_tab, spec, spec_end,
    c_send, c_in, c_out, c_ret, p_spec, y_pieces, o_send, o_in, h_send, h_in,
    prefix, w_light, v_light, gathered, rhs, sums, g_send, g_in,
    halo_s, halo_r, dens_s, dens_r, d_s, d_r, c_s, c_r, b_s, b_r, o_s, o_r, g_s, g_r, h_s, h_r, tab_sem,
):
    S, N, LX, K, VIEWS = sizes
    KP = K // N
    NX, NY = S * LX, N * LANES
    ROWS = KP * LX
    SEG = NX // SEGMENTS
    me = lax.axis_index("sim")
    pe = lax.axis_index("pen")

    def simp(off):
        return lax.rem(me + off + S, S)

    def penp(off):
        return lax.rem(pe + off + N, N)

    def balanced(i, count):
        odd = lax.rem(i, 2)
        half = (i + 1) // 2
        return odd * half + (1 - odd) * (count - half)

    table_copies = [pltpu.make_async_copy(tables_hbm.at[t], q_tab.at[t], tab_sem.at[t]) for t in range(3)]
    for copy in table_copies:
        copy.start()

    barrier = pltpu.get_barrier_semaphore()

    def greet_sim(off, _):
        pl.semaphore_signal(barrier, inc=1, device_id={"sim": simp(off), "pen": pe}, device_id_type=pl.DeviceIdType.MESH)
        return 0

    def greet_pen(off, _):
        pl.semaphore_signal(barrier, inc=1, device_id={"sim": me, "pen": penp(off)}, device_id_type=pl.DeviceIdType.MESH)
        return 0

    lax.fori_loop(1, S, greet_sim, 0)
    lax.fori_loop(1, N, greet_pen, 0)
    corners = ((-1, -1), (-1, 1), (1, -1), (1, 1))
    for dx, dy in corners:
        pl.semaphore_signal(barrier, inc=1, device_id={"sim": simp(dx), "pen": penp(dy)}, device_id_type=pl.DeviceIdType.MESH)

    lane = iota((K, LANES), 1)

    def source(field, x):
        return dens[x] if field == 0 else vel[field - 1, x]

    def pack_body(x, carry):
        first, last = carry
        for field in range(4):
            cells = source(field, x)
            spot = field * LX + x
            here = lane == spot
            first = jnp.where(here, pltpu.roll(cells, spot, 1), first)
            last = jnp.where(here, pltpu.roll(cells, lax.rem(spot + 1, LANES), 1), last)
        return first, last

    nothing = jnp.zeros((K, LANES), f32)
    first, last = lax.fori_loop(0, LX, pack_body, (nothing, nothing), unroll=2)
    pack[0] = first
    pack[1] = last
    for field in range(4):
        pack[2 + field] = source(field, 0)
        pack[6 + field] = source(field, LX - 1)

    pl.semaphore_wait(barrier, (S - 1) + (N - 1) + 4)

    def remote(src, dst, s_sem, r_sem, sim, pen):
        return pltpu.make_async_remote_copy(
            src_ref=src, dst_ref=dst, send_sem=s_sem, recv_sem=r_sem,
            device_id={"sim": sim, "pen": pen}, device_id_type=pl.DeviceIdType.MESH,
        )

    halo = [
        remote(pack.at[pl.ds(6, 4)], xlo, halo_s.at[0], halo_r.at[0], simp(1), pe),
        remote(pack.at[pl.ds(2, 4)], xhi, halo_s.at[1], halo_r.at[1], simp(-1), pe),
    ]
    for side in range(2):
        for dx in (-1, 0, 1):
            slot = side * 3 + 1 + dx
            halo.append(
                remote(
                    pack.at[1 - side], pin.at[slot], halo_s.at[2 + slot], halo_r.at[2 + slot],
                    simp(-dx), penp(1 if side == 0 else -1),
                )
            )
    for copy in halo:
        copy.start()

    def spread_body(x, _):
        for field in range(4):
            cells = source(field, x)
            ext[0, field, x + 1] = pltpu.roll(cells, 1, 1)
            ext[1, field, x + 1] = cells
            ext[2, field, x + 1] = pltpu.roll(cells, LANES - 1, 1)
        return 0

    lax.fori_loop(0, LX, spread_body, 0, unroll=4)
    for copy in halo:
        copy.wait()

    is_first = lane == 0
    is_last = lane == LANES - 1

    def fix_body(x, _):
        for field in range(4):
            spot = field * LX + x
            left = pltpu.roll(pin[1], LANES - spot, 1)
            right = pltpu.roll(pin[4], LANES - 1 - spot, 1)
            ext[0, field, x + 1] = jnp.where(is_first, left, ext[0, field, x + 1])
            ext[2, field, x + 1] = jnp.where(is_last, right, ext[2, field, x + 1])
        return 0

    lax.fori_loop(0, LX, fix_body, 0, unroll=4)
    for row, rows, slot, at in ((0, xlo, 0, LX - 1), (LX + 1, xhi, 2, 0)):
        for field in range(4):
            spot = field * LX + at
            cells = rows[field]
            left = pltpu.roll(pin[slot], (LANES - spot) % LANES, 1)
            right = pltpu.roll(pin[3 + slot], LANES - 1 - spot, 1)
            ext[0, field, row] = jnp.where(is_first, left, pltpu.roll(cells, 1, 1))
            ext[1, field, row] = cells
            ext[2, field, row] = jnp.where(is_last, right, pltpu.roll(cells, LANES - 1, 1))

    def weights(bit, fraction):
        rest = 1.0 - fraction
        on = bit == 1
        return (jnp.where(on, rest, 0.0), jnp.where(on, fraction, rest), jnp.where(on, 0.0, fraction))

    def advect_body(x, _):
        codes = code[x]
        wx = weights(codes & 1, frac[0, x])
        wz = weights((codes >> 1) & 1, frac[1, x])
        wy = weights((codes >> 2) & 1, frac[2, x])
        totals = [None] * 4
        for slot, shift in ((1, 0), (0, -1), (2, 1)):
            if shift == 0:
                rx, ry = wx, wy
            else:
                amount = shift % K
                rx = [pltpu.roll(w, amount, 0) for w in wx]
                ry = [pltpu.roll(w, amount, 0) for w in wy]
            for field in range(4):
                term = None
                for sy in range(3):
                    part = (
                        rx[0] * ext[sy, field, x]
                        + rx[1] * ext[sy, field, x + 1]
                        + rx[2] * ext[sy, field, x + 2]
                    )
                    term = ry[sy] * part if term is None else term + ry[sy] * part
                if shift != 0:
                    term = pltpu.roll(term, (-shift) % K, 0)
                term = wz[slot] * term
                totals[field] = term if totals[field] is None else totals[field] + term
        o_dens[pl.ds(pl.multiple_of(x * K, 8), K), :] = totals[0]
        o_vel[pl.ds(pl.multiple_of(LX * K + x * K, 8), K), :] = totals[2]
        dens_k[pl.ds(x, K, stride=LX), :] = totals[0]
        ax_k[pl.ds(x, K, stride=LX), :] = totals[1]
        ay_k[pl.ds(x, K, stride=LX), :] = totals[3]
        return 0

    lax.fori_loop(0, LX, advect_body, 0)

    def sim_exchange(src, src_rows, dst, s_sem, r_sem):
        def descriptor(peer, start_at):
            a = src.at[pl.ds(pl.multiple_of(peer * src_rows, 8), src_rows)]
            b = dst.at[pl.ds(pl.multiple_of(start_at * src_rows, 8), src_rows)]
            return remote(a, b, s_sem.at[peer], r_sem.at[start_at], peer, pe)

        def start(first=1, end=S):
            def body(i, _):
                descriptor(simp(balanced(i, S)), me).start()
                return 0

            lax.fori_loop(first, end, body, 0)

        def wait_recv():
            def body(off, _):
                peer = simp(off)
                descriptor(peer, peer).wait_recv()
                return 0

            lax.fori_loop(1, S, body, 0)

        def wait_send():
            def body(off, _):
                descriptor(simp(off), me).wait_send()
                return 0

            lax.fori_loop(1, S, body, 0)

        return start, wait_recv, wait_send

    half = N // 2
    near_base = lax.div(pe, half) * half
    far_base = half - near_base

    def pen_exchange(src, dst, s_sem, r_sem):
        def descriptor(peer, start_at):
            return remote(src.at[peer], dst.at[start_at], s_sem.at[peer], r_sem.at[start_at], me, peer)

        def peer_of(i):
            near = near_base + lax.rem(pe - near_base + 1 + i - half, half)
            return jnp.where(i < half, far_base + i, near)

        def loop(method, swap):
            def run(first=0, end=N - 1):
                def body(i, _):
                    peer = peer_of(i)
                    getattr(descriptor(peer, peer if swap else pe), method)()
                    return 0

                lax.fori_loop(first, end, body, 0)

            return run

        return loop("start", False), loop("wait_recv", True), loop("wait_send", False)

    dens_x = sim_exchange(dens_k, LX, rays, dens_s, dens_r)
    early = S // 4
    dens_x[0](1, early)
    mine = pl.ds(pl.multiple_of(me * LX, 8), LX)
    rays[mine, :] = dens_k[mine, :]

    sub_x = iota((LX, LANES), 0)
    lane_x = iota((LX, LANES), 1)

    def div_body(part, _):
        base = part * ROWS
        ends = []
        for layer in range(KP):
            at = pl.ds(pl.multiple_of(base + layer * LX, 8), LX)
            ax = ax_k[at, :]
            ay = ay_k[at, :]
            before_x = jnp.where(sub_x == 0, 0.0, pltpu.roll(ax, 1, 0))
            before_y = jnp.where(lane_x == 0, 0.0, pltpu.roll(ay, 1, 1))
            d_send[part, layer * LX : (layer + 1) * LX, :] = (ax - before_x) + (ay - before_y)
            ends.append(-ax[LX - 1 : LX, :])
        d_send[part, ROWS : ROWS + 8, :] = jnp.concatenate(ends + [jnp.zeros((8 - KP, LANES), f32)], axis=0)
        turned = jnp.transpose(ay_k[pl.ds(pl.multiple_of(base, 8), ROWS), :])
        d_send[part, ROWS + 8 : ROWS + 16, :] = jnp.broadcast_to(turned[LANES - 1 : LANES, :], (8, ROWS))
        return 0

    lax.fori_loop(0, N, div_body, 0)
    d_x = pen_exchange(d_send, d_in, d_s, d_r)
    d_x[0]()
    dens_x[0](early, S)
    d_in[pe] = d_send[pe]
    for copy in table_copies:
        copy.wait()

    lane_r = iota((ROWS, LANES), 1)
    WIDE = half * LANES

    def column_fix(part):
        row = d_in[part, ROWS + 8 : ROWS + 9, :]
        return jnp.where(lane_r == 0, jnp.transpose(jnp.broadcast_to(row, (LANES, ROWS))), 0.0)

    def stage(group, at, cells, end):
        for t, piece in enumerate(split_two(cells)):
            x_pieces[group, t * MSG : t * MSG + ROWS, at] = piece
        for t, piece in enumerate(split_two(end)):
            x_pieces[group, t * MSG + ROWS : (t + 1) * MSG, at] = piece

    def stage_group(group, base):
        for j in range(half):
            cells = d_in[base + j, 0:ROWS, :]
            if j > 0 or group == 1:
                cells = cells - column_fix(lax.rem(base + j - 1 + N, N))
            stage(group, slice(j * LANES, (j + 1) * LANES), cells, d_in[base + j, ROWS:MSG, :])

    def transform(group, base, columns, part_rows):
        wide = 2 * LANES
        rows = pl.ds(pl.multiple_of(base * LANES, LANES), part_rows)

        def body(n, _):
            at = pl.ds(pl.multiple_of(n * wide, wide), wide)
            both = matmul(x_pieces[group, :, columns], q_tab[0, rows, at])
            high = matmul(x_pieces[group, 0:MSG, columns], q_tab[1, rows, at])
            result = both[0:MSG] + (both[MSG : 2 * MSG] + high)
            for side in range(2):
                values = result[:, side * LANES : (side + 1) * LANES]
                line = pl.ds(pl.multiple_of((2 * n + side) * ROWS, 8), ROWS)
                if group == 0:
                    spec[line, :] = values[0:ROWS]
                    spec_end[2 * n + side] = values[ROWS : ROWS + 8]
                else:
                    spec[line, :] = spec[line, :] + values[0:ROWS]
                    spec_end[2 * n + side] = spec_end[2 * n + side] + values[ROWS : ROWS + 8]
            return 0

        lax.fori_loop(0, NY // wide, body, 0)

    d_x[1](half, N - 1)
    stage_group(0, near_base)
    transform(0, near_base, slice(0, WIDE), WIDE)
    d_x[1](0, half)
    stage_group(1, far_base)
    stage(
        1, slice(WIDE, WIDE + LANES), -column_fix(lax.rem(near_base - 1 + N, N)), jnp.zeros((MSG - ROWS, LANES), f32)
    )
    transform(1, far_base, slice(0, WIDE), WIDE)
    transform(1, near_base, slice(WIDE, WIDE + LANES), LANES)

    LINES = N * KP
    root = lines[0]
    root_inv = lines[1]
    beyond = jnp.concatenate([spec_end[part, 0:KP, :] for part in range(N)], axis=0)
    flat = jnp.zeros((LINES, LANES), f32)

    def at_x(x):
        return pl.ds(x, LINES, stride=LX)

    def ends_body(i, carry):
        fwd, bwd, acc = carry
        fwd = spec[at_x(i), :] + root * fwd
        acc = acc + fwd
        bwd = root * (spec[at_x(LX - 1 - i), :] + bwd)
        return fwd, bwd, acc

    fwd, bwd, acc = lax.fori_loop(0, LX, ends_body, (flat, root * beyond, flat), unroll=2)
    fwd = fwd + root_inv * beyond

    def carry_row(row):
        return pl.ds(row, LINES, stride=8)

    c_send[carry_row(0), :] = fwd
    c_send[carry_row(1), :] = bwd
    c_send[carry_row(2), :] = acc
    for row in range(3, 8):
        c_send[carry_row(row), :] = flat
    c_x = sim_exchange(c_send, 8, c_in, c_s, c_r)
    c_x[0]()
    my_carry = pl.ds(pl.multiple_of(me * 8, 8), 8)
    c_in[my_carry, :] = c_send[my_carry, :]

    dens_x[1]()

    def strided(x):
        return pl.ds(x, SEGMENTS, stride=SEG)

    def chain(x):
        return pl.ds(pl.multiple_of(x * SEGMENTS, SEGMENTS), SEGMENTS)

    seg0 = jnp.zeros((SEGMENTS, LANES), f32)

    def scan_body(i, carry):
        depth, down, up = carry
        back = SEG - 1 - i
        glow = ABSORB * rays[strided(i), :]
        prefix[chain(i), :] = depth
        depth = depth + glow
        down = glow + jnp.exp(-glow) * down
        v_light[chain(i), :] = down
        glow_b = ABSORB * rays[strided(back), :]
        up = glow_b + jnp.exp(-glow_b) * up
        w_light[chain(back), :] = up
        return depth, down, up

    seg_depth, seg_down, seg_up = lax.fori_loop(0, SEG, scan_body, (seg0, seg0, seg0), unroll=4)
    seg_pass = jnp.exp(-seg_depth)
    one = jnp.zeros((1, LANES), f32)
    total_depth, run_down, run_up = one, one, one
    starts = []
    for g in range(SEGMENTS):
        starts.append(total_depth)
        total_depth = total_depth + seg_depth[g : g + 1, :]
        run_down = seg_down[g : g + 1, :] + seg_pass[g : g + 1, :] * run_down
        h = SEGMENTS - 1 - g
        run_up = seg_up[h : h + 1, :] + seg_pass[h : h + 1, :] * run_up
    total_pass = jnp.exp(-total_depth)
    closing = 1.0 / (1.0 - total_pass)
    run_down = run_down * closing
    run_up = run_up * closing
    downs, ups = [], []
    for g in range(SEGMENTS):
        downs.append(run_down)
        run_down = seg_down[g : g + 1, :] + seg_pass[g : g + 1, :] * run_down
        h = SEGMENTS - 1 - g
        ups.append(run_up)
        run_up = seg_up[h : h + 1, :] + seg_pass[h : h + 1, :] * run_up
    start_depth = jnp.concatenate(starts, axis=0)
    down_in = jnp.concatenate(downs, axis=0)
    up_in = jnp.concatenate(ups[::-1], axis=0)

    def finish_body(i, _):
        glow = ABSORB * rays[strided(i), :]
        depth = prefix[chain(i), :]
        v_light[chain(i), :] = v_light[chain(i), :] + jnp.exp(-(depth + glow)) * down_in
        w_light[chain(i), :] = w_light[chain(i), :] + jnp.exp(depth - seg_depth) * up_in
        prefix[chain(i), :] = depth + start_depth
        return 0

    lax.fori_loop(0, SEG, finish_body, 0, unroll=4)

    c_x[1]()
    block = lines[4, pl.ds(me, 1), :]
    close = lines[5, pl.ds(me, 1), :]
    lone = jnp.logical_and(iota((1, LANES), 1) == 0, me < KP)

    def carry_at(i, row):
        return pl.ds(8 * i + row, 1)

    def around_body(i, carry):
        a, b = carry
        a = c_in[carry_at(i, 0), :] + block * a
        b = c_in[carry_at(S - 1 - i, 1), :] + block * b
        return a, b

    a, b = lax.fori_loop(0, S, around_body, (one, one))

    def carry_body(i, carry):
        a, b, total = carry
        j = S - 1 - i
        c_out[carry_at(i, 0), :] = a
        c_out[carry_at(j, 1), :] = b
        total = total + (c_in[carry_at(i, 2), :] + LX * a)
        return c_in[carry_at(i, 0), :] + block * a, c_in[carry_at(j, 1), :] + block * b, total

    _, _, total = lax.fori_loop(0, S, carry_body, (a * close, b * close, one))
    mean = total * (1.0 / NX)

    def lone_body(i, offset):
        slope = c_out[carry_at(i, 0), :] - mean
        c_out[carry_at(i, 0), :] = jnp.where(lone, slope, c_out[carry_at(i, 0), :])
        c_out[carry_at(i, 1), :] = jnp.where(lone, offset, c_out[carry_at(i, 1), :])
        return offset + (c_in[carry_at(i, 2), :] + LX * slope)

    lax.fori_loop(0, S, lone_body, one)
    for row in range(2, 8):
        c_out[carry_row(row), :] = flat
    b_x = sim_exchange(c_out, 8, c_ret, b_s, b_r)
    b_x[0]()
    c_ret[my_carry, :] = c_out[my_carry, :]

    sub_v = iota((VIEWS, LANES), 0)
    lane_m = iota((1, 6 * VIEWS), 1)
    view_m = lax.rem(lane_m, VIEWS)

    def where_is(x):
        return lax.rem(x, SEG) * SEGMENTS + lax.div(x, SEG)

    def view_body(v, carry):
        ups_v, start_m, up_m = carry
        x0 = vstart[v]
        up = vsign[v] == 1
        far = jnp.where(up, x0 + STEPS, x0 - STEPS)
        wraps = jnp.logical_or(far >= NX, far < 0)
        xe = jnp.where(far >= NX, far - NX, jnp.where(far < 0, far + NX, far))
        out = []
        for x in (x0, xe):
            at = pl.ds(where_is(x), 1)
            depth = prefix[at, :]
            depth = jnp.where(up, depth, -(depth + ABSORB * rays[pl.ds(x, 1), :]))
            out.append((depth, jnp.where(up, w_light[at, :], v_light[at, :])))
        gathered[0, pl.ds(v, 1), :] = out[0][0]
        gathered[1, pl.ds(v, 1), :] = out[0][1]
        gathered[2, pl.ds(v, 1), :] = out[1][0] + jnp.where(wraps, total_depth, 0.0)
        gathered[3, pl.ds(v, 1), :] = out[1][1]
        flag = vsign[v]
        return (
            jnp.where(sub_v == v, flag, ups_v),
            jnp.where(view_m == v, x0, start_m),
            jnp.where(view_m == v, flag, up_m),
        )

    none_m = jnp.zeros((1, 6 * VIEWS), jnp.int32)
    ups_v, start_m, up_m = lax.fori_loop(0, VIEWS, view_body, (jnp.zeros((VIEWS, LANES), jnp.int32), none_m, none_m))
    entry, light0, leave, light1 = gathered[0], gathered[1], gathered[2], gathered[3]
    seen_through = jnp.exp(entry - leave) * light1
    picture = light0 - seen_through
    o_img[:, 0, :] = picture
    pull = (STEPS * ABSORB) * (picture - targ[:, 0, :])
    coef = pull * jnp.exp(entry)
    alpha = jnp.where(ups_v == 1, coef, 0.0)
    gamma = jnp.where(ups_v == 1, 0.0, coef)
    beta = pull * seen_through
    for slot, value in enumerate((alpha, gamma, beta)):
        wrapped = beta if slot == 2 else value * total_pass
        both = jnp.concatenate([value, wrapped], axis=0)
        for t, piece in enumerate(split_three(both)):
            rhs[t * 2 * VIEWS : (t + 1) * 2 * VIEWS, slot * LANES : (slot + 1) * LANES] = piece

    kind = lax.rem(lax.div(lane_m, VIEWS), 2) == 1
    tile = 256

    def window_body(n, _):
        row = n * tile + iota((tile, 6 * VIEWS), 0)
        x = lax.rem(row, SEGMENTS) * SEG + lax.div(row, SEGMENTS)
        delta = jnp.where(up_m == 1, x - start_m, start_m - x)
        back = delta < 0
        inside = jnp.where(back, delta + NX, delta) < STEPS
        chosen = jnp.logical_and(inside, jnp.logical_xor(back, jnp.logical_not(kind)))
        mask = jnp.where(chosen, 1.0, 0.0).astype(bf16)
        sums[pl.ds(pl.multiple_of(n * tile, tile), tile), :] = matmul(mask, rhs[...])
        return 0

    lax.fori_loop(0, NX // tile, window_body, 0)

    def grad_body(i, _):
        glow = ABSORB * rays[strided(i), :]
        depth = prefix[chain(i), :]
        terms = sums[chain(i), :]
        g_send[strided(i), :] = (
            jnp.exp(-depth) * (1.0 - w_light[chain(i), :] + glow) * terms[:, 0:LANES]
            + jnp.exp(depth + glow) * (1.0 - v_light[chain(i), :] + glow) * terms[:, LANES : 2 * LANES]
            + terms[:, 2 * LANES : 3 * LANES]
        )
        return 0

    lax.fori_loop(0, SEG, grad_body, 0, unroll=4)
    g_x = sim_exchange(g_send, LX, g_in, g_s, g_r)
    g_x[0](1, S // 2)
    g_in[mine, :] = g_send[mine, :]

    b_x[1]()
    factor_f = lines[2]
    factor_b = lines[3]
    alone = jnp.logical_and(iota((LINES, LANES), 1) == 0, iota((LINES, LANES), 0) < KP)
    first_f = c_ret[carry_row(0), :]
    tail = c_ret[carry_row(1), :]
    back_in = tail + root * beyond

    def back_body(i, bwd):
        x = LX - 1 - i
        p_spec[at_x(x), :] = factor_b * bwd
        return root * (spec[at_x(x), :] + bwd)

    lax.fori_loop(0, LX, back_body, back_in, unroll=2)

    def front_body(x, carry):
        fwd, height = carry
        fwd = spec[at_x(x), :] + root * fwd
        p_spec[at_x(x), :] = p_spec[at_x(x), :] + factor_f * jnp.where(alone, height, fwd)
        return fwd, height + fwd

    fwd, height = lax.fori_loop(0, LX, front_body, (first_f, tail), unroll=2)
    after = factor_f * jnp.where(alone, height, root * fwd) + factor_b * (root_inv * back_in)
    for part in range(N):
        at = slice(part * LANES, (part + 1) * LANES)
        for t, piece in enumerate(split_three(p_spec[part * ROWS : (part + 1) * ROWS, :])):
            y_pieces[t * MSG : t * MSG + ROWS, at] = piece
        end = jnp.concatenate([after[part * KP : (part + 1) * KP], jnp.zeros((MSG - ROWS - KP, LANES), f32)], axis=0)
        for t, piece in enumerate(split_three(end)):
            y_pieces[t * MSG + ROWS : (t + 1) * MSG, at] = piece

    def inverse(base):
        def body(n, _):
            wide = PAIR * LANES
            at = pl.ds(pl.multiple_of(base * LANES + n * wide, LANES), wide)
            first = matmul(y_pieces[...], q_tab[0, :, at])
            second = matmul(y_pieces[0 : 2 * MSG], q_tab[1, :, at])
            third = matmul(y_pieces[0:MSG], q_tab[2, :, at])
            small = second[MSG : 2 * MSG] + third + first[2 * MSG : 3 * MSG]
            result = first[0:MSG] + (first[MSG : 2 * MSG] + second[0:MSG] + small)
            for side in range(PAIR):
                o_send[base + PAIR * n + side] = result[:, side * LANES : (side + 1) * LANES]
            return 0

        lax.fori_loop(0, half // PAIR, body, 0)

    PAIR = min(2, half)
    o_x = pen_exchange(o_send, o_in, o_s, o_r)
    inverse(far_base)
    o_x[0](0, half)
    inverse(near_base)
    o_x[0](half, N - 1)
    for part in range(N):
        turned = jnp.transpose(o_send[(part + 1) % N, 0:ROWS, :])
        h_send[part] = jnp.broadcast_to(turned[0:1, :], (8, ROWS))
    h_x = pen_exchange(h_send, h_in, h_s, h_r)
    h_x[0]()
    g_x[0](S // 2, S)
    o_in[pe] = o_send[pe]
    h_in[pe] = h_send[pe]

    def velocity_part(part):
        column = jnp.transpose(jnp.broadcast_to(h_in[part, 0:1, :], (LANES, ROWS)))
        for layer in range(KP):
            k = part * KP + layer
            at = pl.ds(pl.multiple_of(k * LX, 8), LX)
            here = o_in[part, layer * LX : (layer + 1) * LX, :]
            above = o_in[part, ROWS + layer : ROWS + layer + 1, :]
            next_x = jnp.where(sub_x == LX - 1, above, pltpu.roll(here, LX - 1, 0))
            next_y = jnp.where(
                lane_x == LANES - 1, column[layer * LX : (layer + 1) * LX, :], pltpu.roll(here, LANES - 1, 1)
            )
            o_vel[pl.ds(k, LX, stride=K), :] = ax_k[at, :] - (next_x - here)
            o_vel[pl.ds(2 * LX * K + k, LX, stride=K), :] = ay_k[at, :] - (next_y - here)

    def velocity_group(base):
        def body(j, _):
            velocity_part(base + j)
            return 0

        lax.fori_loop(0, half, body, 0)

    o_x[1](half, N - 1)
    h_x[1](half, N - 1)
    velocity_group(near_base)
    o_x[1](0, half)
    h_x[1](0, half)
    velocity_group(far_base)

    g_x[1]()

    def back_home(k, _):
        o_grad[pl.ds(k, LX, stride=K), :] = g_in[pl.ds(pl.multiple_of(k * LX, 8), LX), :]
        return 0

    lax.fori_loop(0, K, back_home, 0)
    for copy_sends in (dens_x[2], d_x[2], c_x[2], b_x[2], g_x[2], o_x[2], h_x[2]):
        copy_sends()


def hand_over(*refs):
    count = (len(refs) - 2) // 3
    sources, targets, rooms = refs[:count], refs[count : 2 * count], refs[2 * count : 3 * count]
    in_sem, out_sem = refs[3 * count :]
    blocks = []
    for source, target, room in zip(sources, targets, rooms):
        rows = source.shape[0]
        size = min(rows, 512)
        for at in range(0, rows, size):
            part = pl.ds(at, size)
            slot = len(blocks)
            blocks.append(
                (
                    pltpu.make_async_copy(source.at[part], room.at[part], in_sem.at[slot]),
                    pltpu.make_async_copy(room.at[part], target.at[part], out_sem.at[slot]),
                )
            )
    for fetch, _ in blocks:
        fetch.start()
    for fetch, store in blocks:
        fetch.wait()
        store.start()
    for _, store in blocks:
        store.wait()


def solution(mesh):
    S, N = mesh.shape["sim"], mesh.shape["pen"]

    def shards(density, velocity, stencil_code, fractions, targets, view_start, view_sign):
        LX, K, LY = density.shape
        VIEWS = targets.shape[0]
        NX, NY = LX * S, LY * N
        tables = jnp.asarray(hartley_pieces(NY))
        lines = jnp.asarray(line_tables(NY, NX, LX, K // N))
        vmem = pl.BlockSpec(memory_space=pltpu.VMEM)
        smem = pl.BlockSpec(memory_space=pltpu.SMEM)
        dma = pltpu.SemaphoreType.DMA
        scratch = [
            pltpu.VMEM((3, 4, LX + 2, K, LY), f32),
            pltpu.VMEM((10, K, LY), f32),
            pltpu.VMEM((4, K, LY), f32),
            pltpu.VMEM((4, K, LY), f32),
            pltpu.VMEM((6, K, LY), f32),
            pltpu.VMEM((K * LX, LY), f32),
            pltpu.VMEM((K * LX, LY), f32),
            pltpu.VMEM((K * LX, LY), f32),
            pltpu.VMEM((NX, LY), f32),
            pltpu.VMEM((N, MSG, LY), f32),
            pltpu.VMEM((N, MSG, LY), f32),
            pltpu.VMEM((2, 2 * MSG, NY // 2 + LANES), bf16),
            pltpu.VMEM((3, NY, NY), bf16),
            pltpu.VMEM((N * 128, LANES), f32),
            pltpu.VMEM((N, 8, LANES), f32),
            pltpu.VMEM((S * 8, LANES), f32),
            pltpu.VMEM((S * 8, LANES), f32),
            pltpu.VMEM((S * 8, LANES), f32),
            pltpu.VMEM((S * 8, LANES), f32),
            pltpu.VMEM((N * 128, LANES), f32),
            pltpu.VMEM((3 * MSG, NY), bf16),
            pltpu.VMEM((N, MSG, LY), f32),
            pltpu.VMEM((N, MSG, LY), f32),
            pltpu.VMEM((N, 8, LY), f32),
            pltpu.VMEM((N, 8, LY), f32),
            pltpu.VMEM((NX, LY), f32),
            pltpu.VMEM((NX, LY), f32),
            pltpu.VMEM((NX, LY), f32),
            pltpu.VMEM((4, VIEWS, LY), f32),
            pltpu.VMEM((6 * VIEWS, 3 * LY), bf16),
            pltpu.VMEM((NX, 3 * LY), f32),
            pltpu.VMEM((NX, LY), f32),
            pltpu.VMEM((K * LX, LY), f32),
            dma((8,)), dma((8,)),
            dma((S,)), dma((S,)),
            dma((N,)), dma((N,)),
            dma((S,)), dma((S,)),
            dma((S,)), dma((S,)),
            dma((N,)), dma((N,)),
            dma((S,)), dma((S,)),
            dma((N,)), dma((N,)),
            dma((3,)),
        ]
        density_new, velocity_new, images, gradient = pl.pallas_call(
            functools.partial(step_kernel, (S, N, LX, K, VIEWS)),
            out_shape=(
                jax.ShapeDtypeStruct((LX * K, LY), f32),
                jax.ShapeDtypeStruct((3 * LX * K, LY), f32),
                jax.ShapeDtypeStruct(targets.shape, f32),
                jax.ShapeDtypeStruct((LX * K, LY), f32),
            ),
            in_specs=[vmem, vmem, vmem, vmem, vmem, smem, smem, pl.BlockSpec(memory_space=pl.ANY), vmem],
            out_specs=(vmem, vmem, vmem, vmem),
            scratch_shapes=scratch,
            compiler_params=pltpu.CompilerParams(
                collective_id=0, has_side_effects=True, vmem_limit_bytes=60 * 1024 * 1024
            ),
        )(density, velocity, stencil_code, fractions, targets, view_start, view_sign, tables, lines)
        results = (density_new, velocity_new, images, gradient)
        shapes = tuple(jax.ShapeDtypeStruct(value.shape, value.dtype) for value in results)
        anywhere = pl.BlockSpec(memory_space=pl.ANY)
        density_new, velocity_new, images, gradient = pl.pallas_call(
            hand_over,
            out_shape=shapes,
            in_specs=[anywhere] * 4,
            out_specs=(anywhere,) * 4,
            scratch_shapes=[pltpu.VMEM(shape.shape, f32) for shape in shapes] + [dma((32,)), dma((32,))],
            compiler_params=pltpu.CompilerParams(vmem_limit_bytes=60 * 1024 * 1024),
        )(*results)
        return (
            density_new.reshape(LX, K, LY),
            velocity_new.reshape(3, LX, K, LY),
            images,
            gradient.reshape(LX, K, LY),
        )

    return jax.shard_map(
        shards,
        mesh=mesh,
        in_specs=(
            P("sim", None, "pen"),
            P(None, "sim", None, "pen"),
            P("sim", None, "pen"),
            P(None, "sim", None, "pen"),
            P(None, "sim", "pen"),
            P(),
            P(),
        ),
        out_specs=(
            P("sim", None, "pen"),
            P(None, "sim", None, "pen"),
            P(None, "sim", "pen"),
            P("sim", None, "pen"),
        ),
        check_vma=False,
    )
```

```python
import functools

import jax
import jax.numpy as jnp
import numpy as np
from jax import lax
from jax.experimental import pallas as pl
from jax.experimental.pallas import tpu as pltpu
from jax.sharding import PartitionSpec as P

STEPS = 256
ABSORB = 2.0 / STEPS
LANES = 128
SEGMENTS = 8
MSG = 144
f32 = jnp.float32
bf16 = jnp.bfloat16


def hartley_pieces(length):
    index = np.arange(length)
    angles = (np.outer(index, index) % length) * (2.0 * np.pi / length)
    table = (np.cos(angles) + np.sin(angles)) / np.sqrt(length)
    pieces = []
    for _ in range(3):
        piece = table.astype(jnp.bfloat16)
        pieces.append(piece)
        table = table - piece.astype(np.float64)
    return np.stack(pieces)


def line_tables(length_y, length_x, local_x, layers):
    eig = 4.0 * np.sin(np.pi * np.arange(length_y) / length_y) ** 2
    half = eig / 2.0
    root = 1.0 / (1.0 + half + np.sqrt(half * (half + 2.0)))
    gap = 1.0 / root - root
    gap[0] = 1.0
    forward = -1.0 / gap
    backward = -1.0 / gap
    forward[0] = 1.0
    backward[0] = 0.0
    block = root**local_x
    closing = 1.0 - root**length_x
    closing[0] = 1.0
    closing = 1.0 / closing
    closing[0] = 0.0
    rows = np.stack([root, 1.0 / root, forward, backward, block, closing])
    rows = rows.reshape(6, length_y // LANES, 1, LANES)
    return np.repeat(rows, layers, axis=2).reshape(6, -1, LANES).astype(np.float32)


def split_two(values):
    high = values.astype(bf16)
    low = (values - high.astype(f32)).astype(bf16)
    return high, low


def split_three(values):
    high = values.astype(bf16)
    rest = values - high.astype(f32)
    mid = rest.astype(bf16)
    low = (rest - mid.astype(f32)).astype(bf16)
    return high, mid, low


def iota(shape, dim):
    return lax.broadcasted_iota(jnp.int32, shape, dim)


def matmul(a, b):
    return jnp.dot(a, b, preferred_element_type=f32)


def step_kernel(
    sizes,
    dens_hbm, vel_hbm, code_hbm, frac_hbm, targ, vstart, vsign, tables_hbm, lines,
    o_dens_hbm, o_vel_hbm, o_img, o_grad_hbm,
    dens, vel, code, frac, o_dens, o_vel, o_grad, io_sem,
    ext, pack, xlo, xhi, pin, dens_k, ax_k, ay_k,
    rays, d_send, d_in, x_pieces, q_tab, spec, spec_end,
    c_send, c_in, c_out, c_ret, ends, p_spec, y_pieces, o_send, o_in, h_send, h_in,
    prefix, w_light, v_light, gathered, rhs, sums, g_send, g_in,
    halo_s, halo_r, dens_s, dens_r, d_s, d_r, c_s, c_r, b_s, b_r, o_s, o_r, g_s, g_r, h_s, h_r, tab_sem,
):
    S, N, LX, K, VIEWS = sizes
    KP = K // N
    NX, NY = S * LX, N * LANES
    ROWS = KP * LX
    SEG = NX // SEGMENTS
    me = lax.axis_index("sim")
    pe = lax.axis_index("pen")

    def simp(off):
        return lax.rem(me + off + S, S)

    def penp(off):
        return lax.rem(pe + off + N, N)

    def balanced(i, count):
        odd = lax.rem(i, 2)
        half = (i + 1) // 2
        return odd * half + (1 - odd) * (count - half)

    parts = LX // 2
    fields_in = [pltpu.make_async_copy(dens_hbm.at[pl.ds(h * parts, parts)], dens.at[pl.ds(h * parts, parts)], io_sem.at[h]) for h in range(2)]
    fields_in += [
        pltpu.make_async_copy(vel_hbm.at[c, pl.ds(h * parts, parts)], vel.at[c, pl.ds(h * parts, parts)], io_sem.at[2 + 2 * c + h])
        for c in range(3)
        for h in range(2)
    ]
    weights_in = [pltpu.make_async_copy(code_hbm, code, io_sem.at[8])]
    weights_in += [pltpu.make_async_copy(frac_hbm.at[c], frac.at[c], io_sem.at[9 + c]) for c in range(3)]
    for copy in fields_in + weights_in:
        copy.start()
    table_copies = [pltpu.make_async_copy(tables_hbm.at[t], q_tab.at[t], tab_sem.at[t]) for t in range(3)]
    for copy in table_copies:
        copy.start()

    barrier = pltpu.get_barrier_semaphore()

    def greet_sim(off, _):
        pl.semaphore_signal(barrier, inc=1, device_id={"sim": simp(off), "pen": pe}, device_id_type=pl.DeviceIdType.MESH)
        return 0

    def greet_pen(off, _):
        pl.semaphore_signal(barrier, inc=1, device_id={"sim": me, "pen": penp(off)}, device_id_type=pl.DeviceIdType.MESH)
        return 0

    lax.fori_loop(1, S, greet_sim, 0)
    lax.fori_loop(1, N, greet_pen, 0)
    corners = ((-1, -1), (-1, 1), (1, -1), (1, 1))
    for dx, dy in corners:
        pl.semaphore_signal(barrier, inc=1, device_id={"sim": simp(dx), "pen": penp(dy)}, device_id_type=pl.DeviceIdType.MESH)

    for copy in fields_in:
        copy.wait()

    lane = iota((K, LANES), 1)

    def source(field, x):
        return dens[x] if field == 0 else vel[field - 1, x]

    def pack_body(x, carry):
        first, last = carry
        for field in range(4):
            cells = source(field, x)
            spot = field * LX + x
            here = lane == spot
            first = jnp.where(here, pltpu.roll(cells, spot, 1), first)
            last = jnp.where(here, pltpu.roll(cells, lax.rem(spot + 1, LANES), 1), last)
        return first, last

    nothing = jnp.zeros((K, LANES), f32)
    first, last = lax.fori_loop(0, LX, pack_body, (nothing, nothing), unroll=4)
    pack[0] = first
    pack[1] = last
    for field in range(4):
        pack[2 + field] = source(field, 0)
        pack[6 + field] = source(field, LX - 1)

    pl.semaphore_wait(barrier, (S - 1) + (N - 1) + 4)

    def remote(src, dst, s_sem, r_sem, sim, pen):
        return pltpu.make_async_remote_copy(
            src_ref=src, dst_ref=dst, send_sem=s_sem, recv_sem=r_sem,
            device_id={"sim": sim, "pen": pen}, device_id_type=pl.DeviceIdType.MESH,
        )

    halo = [
        remote(pack.at[pl.ds(6, 4)], xlo, halo_s.at[0], halo_r.at[0], simp(1), pe),
        remote(pack.at[pl.ds(2, 4)], xhi, halo_s.at[1], halo_r.at[1], simp(-1), pe),
    ]
    for side in range(2):
        for dx in (-1, 0, 1):
            slot = side * 3 + 1 + dx
            halo.append(
                remote(
                    pack.at[1 - side], pin.at[slot], halo_s.at[2 + slot], halo_r.at[2 + slot],
                    simp(-dx), penp(1 if side == 0 else -1),
                )
            )
    for copy in halo:
        copy.start()

    def spread_body(x, _):
        for field in range(4):
            cells = source(field, x)
            ext[0, field, x + 1] = pltpu.roll(cells, 1, 1)
            ext[1, field, x + 1] = cells
            ext[2, field, x + 1] = pltpu.roll(cells, LANES - 1, 1)
        return 0

    lax.fori_loop(0, LX, spread_body, 0, unroll=4)
    for copy in halo:
        copy.wait()

    is_first = lane == 0
    is_last = lane == LANES - 1

    def fix_body(x, _):
        for field in range(4):
            spot = field * LX + x
            left = pltpu.roll(pin[1], LANES - spot, 1)
            right = pltpu.roll(pin[4], LANES - 1 - spot, 1)
            ext[0, field, x + 1] = jnp.where(is_first, left, ext[0, field, x + 1])
            ext[2, field, x + 1] = jnp.where(is_last, right, ext[2, field, x + 1])
        return 0

    lax.fori_loop(0, LX, fix_body, 0, unroll=8)
    for row, rows, slot, at in ((0, xlo, 0, LX - 1), (LX + 1, xhi, 2, 0)):
        for field in range(4):
            spot = field * LX + at
            cells = rows[field]
            left = pltpu.roll(pin[slot], (LANES - spot) % LANES, 1)
            right = pltpu.roll(pin[3 + slot], LANES - 1 - spot, 1)
            ext[0, field, row] = jnp.where(is_first, left, pltpu.roll(cells, 1, 1))
            ext[1, field, row] = cells
            ext[2, field, row] = jnp.where(is_last, right, pltpu.roll(cells, LANES - 1, 1))

    for copy in weights_in:
        copy.wait()

    def weights(bit, fraction):
        rest = 1.0 - fraction
        on = bit == 1
        return (jnp.where(on, rest, 0.0), jnp.where(on, fraction, rest), jnp.where(on, 0.0, fraction))

    def advect_body(x, _):
        codes = code[x]
        wx = weights(codes & 1, frac[0, x])
        wz = weights((codes >> 1) & 1, frac[1, x])
        wy = weights((codes >> 2) & 1, frac[2, x])
        totals = [None] * 4
        for slot, shift in ((1, 0), (0, -1), (2, 1)):
            if shift == 0:
                rx, ry = wx, wy
            else:
                amount = shift % K
                rx = [pltpu.roll(w, amount, 0) for w in wx]
                ry = [pltpu.roll(w, amount, 0) for w in wy]
            for field in range(4):
                term = None
                for sy in range(3):
                    part = (
                        rx[0] * ext[sy, field, x]
                        + rx[1] * ext[sy, field, x + 1]
                        + rx[2] * ext[sy, field, x + 2]
                    )
                    term = ry[sy] * part if term is None else term + ry[sy] * part
                if shift != 0:
                    term = pltpu.roll(term, (-shift) % K, 0)
                term = wz[slot] * term
                totals[field] = term if totals[field] is None else totals[field] + term
        o_dens[pl.ds(pl.multiple_of(x * K, 8), K), :] = totals[0]
        o_vel[pl.ds(pl.multiple_of(LX * K + x * K, 8), K), :] = totals[2]
        dens_k[pl.ds(x, K, stride=LX), :] = totals[0]
        ax_k[pl.ds(x, K, stride=LX), :] = totals[1]
        ay_k[pl.ds(x, K, stride=LX), :] = totals[3]
        return 0

    lax.fori_loop(0, LX, advect_body, 0)
    block = LX * K
    stores = [
        pltpu.make_async_copy(o_dens, o_dens_hbm, io_sem.at[12]),
        pltpu.make_async_copy(o_vel.at[pl.ds(block, block)], o_vel_hbm.at[pl.ds(block, block)], io_sem.at[13]),
    ]
    for copy in stores:
        copy.start()

    def sim_exchange(src, src_rows, dst, s_sem, r_sem):
        def descriptor(peer, start_at):
            if src_rows:
                a = src.at[pl.ds(pl.multiple_of(peer * src_rows, 8), src_rows)]
                b = dst.at[pl.ds(pl.multiple_of(start_at * src_rows, 8), src_rows)]
            else:
                a, b = src.at[peer], dst.at[start_at]
            return remote(a, b, s_sem.at[peer], r_sem.at[start_at], peer, pe)

        def start(first=1, end=S):
            def body(i, _):
                descriptor(simp(balanced(i, S)), me).start()
                return 0

            lax.fori_loop(first, end, body, 0)

        def wait_recv():
            def body(off, _):
                peer = simp(off)
                descriptor(peer, peer).wait_recv()
                return 0

            lax.fori_loop(1, S, body, 0)

        def wait_send():
            def body(off, _):
                descriptor(simp(off), me).wait_send()
                return 0

            lax.fori_loop(1, S, body, 0)

        return start, wait_recv, wait_send

    half = N // 2
    near_base = lax.div(pe, half) * half
    far_base = half - near_base

    def pen_peer(i):
        near = near_base + lax.rem(pe - near_base + 1 + i, half)
        return jnp.where(i < half, far_base + i, near)

    def pen_exchange(src, dst, s_sem, r_sem):
        def descriptor(peer, start_at):
            return remote(src.at[peer], dst.at[start_at], s_sem.at[peer], r_sem.at[start_at], me, peer)

        def loop(method, swap):
            def run(first=0, end=N - 1):
                def body(i, _):
                    peer = pen_peer(i)
                    getattr(descriptor(peer, peer if swap else pe), method)()
                    return 0

                lax.fori_loop(first, end, body, 0)

            return run

        return loop("start", False), loop("wait_recv", True), loop("wait_send", False)

    dens_x = sim_exchange(dens_k, LX, rays, dens_s, dens_r)
    early = S // 4
    dens_x[0](1, early)
    mine = pl.ds(pl.multiple_of(me * LX, 8), LX)
    rays[mine, :] = dens_k[mine, :]

    sub_x = iota((LX, LANES), 0)
    lane_x = iota((LX, LANES), 1)

    def div_part(part):
        base = part * ROWS
        ends = []
        for layer in range(KP):
            at = pl.ds(pl.multiple_of(base + layer * LX, 8), LX)
            ax = ax_k[at, :]
            ay = ay_k[at, :]
            before_x = jnp.where(sub_x == 0, 0.0, pltpu.roll(ax, 1, 0))
            before_y = jnp.where(lane_x == 0, 0.0, pltpu.roll(ay, 1, 1))
            d_send[part, layer * LX : (layer + 1) * LX, :] = (ax - before_x) + (ay - before_y)
            ends.append(-ax[LX - 1 : LX, :])
        d_send[part, ROWS : ROWS + 8, :] = jnp.concatenate(ends + [jnp.zeros((8 - KP, LANES), f32)], axis=0)
        turned = jnp.transpose(ay_k[pl.ds(pl.multiple_of(base, 8), ROWS), :])
        d_send[part, ROWS + 8 : ROWS + 16, :] = jnp.broadcast_to(turned[LANES - 1 : LANES, :], (8, ROWS))

    d_x = pen_exchange(d_send, d_in, d_s, d_r)

    def div_send(i, _):
        div_part(pen_peer(i))
        d_x[0](i, i + 1)
        return 0

    lax.fori_loop(0, N - 1, div_send, 0)
    div_part(pe)
    dens_x[0](early, S)
    d_in[pe] = d_send[pe]
    for copy in table_copies:
        copy.wait()

    lane_r = iota((ROWS, LANES), 1)
    WIDE = half * LANES

    def column_fix(part):
        row = d_in[part, ROWS + 8 : ROWS + 9, :]
        return jnp.where(lane_r == 0, jnp.transpose(jnp.broadcast_to(row, (LANES, ROWS))), 0.0)

    def stage(group, at, cells, end):
        for t, piece in enumerate(split_two(cells)):
            x_pieces[group, t * MSG : t * MSG + ROWS, at] = piece
        for t, piece in enumerate(split_two(end)):
            x_pieces[group, t * MSG + ROWS : (t + 1) * MSG, at] = piece

    def stage_group(group, base):
        for j in range(half):
            cells = d_in[base + j, 0:ROWS, :]
            if j > 0 or group == 1:
                cells = cells - column_fix(lax.rem(base + j - 1 + N, N))
            stage(group, slice(j * LANES, (j + 1) * LANES), cells, d_in[base + j, ROWS:MSG, :])

    def transform(group, base, columns, part_rows):
        wide = 2 * LANES
        rows = pl.ds(pl.multiple_of(base * LANES, LANES), part_rows)

        def body(n, _):
            at = pl.ds(pl.multiple_of(n * wide, wide), wide)
            both = matmul(x_pieces[group, :, columns], q_tab[0, rows, at])
            high = matmul(x_pieces[group, 0:MSG, columns], q_tab[1, rows, at])
            result = both[0:MSG] + (both[MSG : 2 * MSG] + high)
            for side in range(2):
                values = result[:, side * LANES : (side + 1) * LANES]
                line = pl.ds(pl.multiple_of((2 * n + side) * ROWS, 8), ROWS)
                if group == 0:
                    spec[line, :] = values[0:ROWS]
                    spec_end[2 * n + side] = values[ROWS : ROWS + 8]
                else:
                    spec[line, :] = spec[line, :] + values[0:ROWS]
                    spec_end[2 * n + side] = spec_end[2 * n + side] + values[ROWS : ROWS + 8]
            return 0

        lax.fori_loop(0, NY // wide, body, 0)

    d_x[1](half, N - 1)
    stage_group(0, near_base)
    transform(0, near_base, slice(0, WIDE), WIDE)
    d_x[1](0, half)
    stage_group(1, far_base)
    stage(
        1, slice(WIDE, WIDE + LANES), -column_fix(lax.rem(near_base - 1 + N, N)), jnp.zeros((MSG - ROWS, LANES), f32)
    )
    transform(1, far_base, slice(0, WIDE), WIDE)
    transform(1, near_base, slice(WIDE, WIDE + LANES), LANES)

    LINES = N * KP
    root = lines[0]
    root_inv = lines[1]
    beyond = jnp.concatenate([spec_end[part, 0:KP, :] for part in range(N)], axis=0)
    flat = jnp.zeros((LINES, LANES), f32)

    def at_x(x):
        return pl.ds(x, LINES, stride=LX)

    def ends_body(i, carry):
        fwd, bwd, acc = carry
        fwd = spec[at_x(i), :] + root * fwd
        acc = acc + fwd
        bwd = root * (spec[at_x(LX - 1 - i), :] + bwd)
        return fwd, bwd, acc

    fwd, bwd, acc = lax.fori_loop(0, LX, ends_body, (flat, root * beyond, flat), unroll=2)
    fwd = fwd + root_inv * beyond

    alone = jnp.logical_and(iota((LINES, LANES), 1) == 0, iota((LINES, LANES), 0) < KP)
    bwd = jnp.where(alone, acc, bwd)
    for line in range(LINES):
        c_send[line, 0:1, :] = fwd[line : line + 1]
        c_send[line, 1:2, :] = bwd[line : line + 1]
    c_x = sim_exchange(c_send, 0, c_in, c_s, c_r)
    c_x[0]()
    c_in[me] = c_send[me]

    dens_x[1]()

    def strided(x):
        return pl.ds(x, SEGMENTS, stride=SEG)

    def chain(x):
        return pl.ds(pl.multiple_of(x * SEGMENTS, SEGMENTS), SEGMENTS)

    seg0 = jnp.zeros((SEGMENTS, LANES), f32)

    def scan_body(i, carry):
        depth, down, up = carry
        back = SEG - 1 - i
        glow = ABSORB * rays[strided(i), :]
        prefix[chain(i), :] = depth
        depth = depth + glow
        down = glow + jnp.exp(-glow) * down
        v_light[chain(i), :] = down
        glow_b = ABSORB * rays[strided(back), :]
        up = glow_b + jnp.exp(-glow_b) * up
        w_light[chain(back), :] = up
        return depth, down, up

    seg_depth, seg_down, seg_up = lax.fori_loop(0, SEG, scan_body, (seg0, seg0, seg0), unroll=4)
    seg_pass = jnp.exp(-seg_depth)
    one = jnp.zeros((1, LANES), f32)
    total_depth, run_down, run_up = one, one, one
    starts = []
    for g in range(SEGMENTS):
        starts.append(total_depth)
        total_depth = total_depth + seg_depth[g : g + 1, :]
        run_down = seg_down[g : g + 1, :] + seg_pass[g : g + 1, :] * run_down
        h = SEGMENTS - 1 - g
        run_up = seg_up[h : h + 1, :] + seg_pass[h : h + 1, :] * run_up
    total_pass = jnp.exp(-total_depth)
    closing = 1.0 / (1.0 - total_pass)
    run_down = run_down * closing
    run_up = run_up * closing
    downs, ups = [], []
    for g in range(SEGMENTS):
        downs.append(run_down)
        run_down = seg_down[g : g + 1, :] + seg_pass[g : g + 1, :] * run_down
        h = SEGMENTS - 1 - g
        ups.append(run_up)
        run_up = seg_up[h : h + 1, :] + seg_pass[h : h + 1, :] * run_up
    start_depth = jnp.concatenate(starts, axis=0)
    down_in = jnp.concatenate(downs, axis=0)
    up_in = jnp.concatenate(ups[::-1], axis=0)

    def finish_body(i, _):
        glow = ABSORB * rays[strided(i), :]
        depth = prefix[chain(i), :]
        v_light[chain(i), :] = v_light[chain(i), :] + jnp.exp(-(depth + glow)) * down_in
        w_light[chain(i), :] = w_light[chain(i), :] + jnp.exp(depth - seg_depth) * up_in
        prefix[chain(i), :] = depth + start_depth
        return 0

    lax.fori_loop(0, SEG, finish_body, 0, unroll=4)

    c_x[1]()
    power = lines[4, pl.ds(me, 1), :]
    close = lines[5, pl.ds(me, 1), :]
    lone = jnp.logical_and(iota((1, LANES), 1) == 0, me < KP)

    def around_body(i, carry):
        a, b = carry
        a = c_in[i, 0:1, :] + power * a
        b = c_in[S - 1 - i, 1:2, :] + power * b
        return a, b

    a, b = lax.fori_loop(0, S, around_body, (one, one))

    def carry_body(i, carry):
        a, b, total = carry
        j = S - 1 - i
        c_out[i, 0:1, :] = a
        c_out[j, 1:2, :] = b
        total = total + (c_in[i, 1:2, :] + LX * a)
        return c_in[i, 0:1, :] + power * a, c_in[j, 1:2, :] + power * b, total

    _, _, total = lax.fori_loop(0, S, carry_body, (a * close, b * close, one))
    mean = total * (1.0 / NX)

    def lone_body(i, offset):
        slope = c_out[i, 0:1, :] - mean
        c_out[i, 0:1, :] = jnp.where(lone, slope, c_out[i, 0:1, :])
        c_out[i, 1:2, :] = jnp.where(lone, offset, c_out[i, 1:2, :])
        return offset + (c_in[i, 1:2, :] + LX * slope)

    lax.fori_loop(0, S, lone_body, one)
    b_x = sim_exchange(c_out, 0, c_ret, b_s, b_r)
    b_x[0]()
    c_ret[me] = c_out[me]

    sub_v = iota((VIEWS, LANES), 0)
    lane_m = iota((1, 6 * VIEWS), 1)
    view_m = lax.rem(lane_m, VIEWS)

    def where_is(x):
        return lax.rem(x, SEG) * SEGMENTS + lax.div(x, SEG)

    def view_body(v, carry):
        ups_v, start_m, up_m = carry
        x0 = vstart[v]
        up = vsign[v] == 1
        far = jnp.where(up, x0 + STEPS, x0 - STEPS)
        wraps = jnp.logical_or(far >= NX, far < 0)
        xe = jnp.where(far >= NX, far - NX, jnp.where(far < 0, far + NX, far))
        out = []
        for x in (x0, xe):
            at = pl.ds(where_is(x), 1)
            depth = prefix[at, :]
            depth = jnp.where(up, depth, -(depth + ABSORB * rays[pl.ds(x, 1), :]))
            out.append((depth, jnp.where(up, w_light[at, :], v_light[at, :])))
        gathered[0, pl.ds(v, 1), :] = out[0][0]
        gathered[1, pl.ds(v, 1), :] = out[0][1]
        gathered[2, pl.ds(v, 1), :] = out[1][0] + jnp.where(wraps, total_depth, 0.0)
        gathered[3, pl.ds(v, 1), :] = out[1][1]
        flag = vsign[v]
        return (
            jnp.where(sub_v == v, flag, ups_v),
            jnp.where(view_m == v, x0, start_m),
            jnp.where(view_m == v, flag, up_m),
        )

    none_m = jnp.zeros((1, 6 * VIEWS), jnp.int32)
    ups_v, start_m, up_m = lax.fori_loop(0, VIEWS, view_body, (jnp.zeros((VIEWS, LANES), jnp.int32), none_m, none_m))
    entry, light0, leave, light1 = gathered[0], gathered[1], gathered[2], gathered[3]
    seen_through = jnp.exp(entry - leave) * light1
    picture = light0 - seen_through
    o_img[:, 0, :] = picture
    pull = (STEPS * ABSORB) * (picture - targ[:, 0, :])
    coef = pull * jnp.exp(entry)
    alpha = jnp.where(ups_v == 1, coef, 0.0)
    gamma = jnp.where(ups_v == 1, 0.0, coef)
    beta = pull * seen_through
    for slot, value in enumerate((alpha, gamma, beta)):
        wrapped = beta if slot == 2 else value * total_pass
        both = jnp.concatenate([value, wrapped], axis=0)
        for t, piece in enumerate(split_three(both)):
            rhs[t * 2 * VIEWS : (t + 1) * 2 * VIEWS, slot * LANES : (slot + 1) * LANES] = piece

    kind = lax.rem(lax.div(lane_m, VIEWS), 2) == 1
    tile = 256

    def window_body(n, _):
        row = n * tile + iota((tile, 6 * VIEWS), 0)
        x = lax.rem(row, SEGMENTS) * SEG + lax.div(row, SEGMENTS)
        delta = jnp.where(up_m == 1, x - start_m, start_m - x)
        back = delta < 0
        inside = jnp.where(back, delta + NX, delta) < STEPS
        chosen = jnp.logical_and(inside, jnp.logical_xor(back, jnp.logical_not(kind)))
        mask = jnp.where(chosen, 1.0, 0.0).astype(bf16)
        sums[pl.ds(pl.multiple_of(n * tile, tile), tile), :] = matmul(mask, rhs[...])
        return 0

    lax.fori_loop(0, NX // tile, window_body, 0)

    def grad_body(i, _):
        glow = ABSORB * rays[strided(i), :]
        depth = prefix[chain(i), :]
        terms = sums[chain(i), :]
        g_send[strided(i), :] = (
            jnp.exp(-depth) * (1.0 - w_light[chain(i), :] + glow) * terms[:, 0:LANES]
            + jnp.exp(depth + glow) * (1.0 - v_light[chain(i), :] + glow) * terms[:, LANES : 2 * LANES]
            + terms[:, 2 * LANES : 3 * LANES]
        )
        return 0

    lax.fori_loop(0, SEG, grad_body, 0, unroll=4)
    g_x = sim_exchange(g_send, LX, g_in, g_s, g_r)
    g_x[0](1, S // 2)
    g_in[mine, :] = g_send[mine, :]

    b_x[1]()
    factor_f = lines[2]
    factor_b = lines[3]
    for line in range(LINES):
        ends[0, line : line + 1, :] = c_ret[line, 0:1, :]
        ends[1, line : line + 1, :] = c_ret[line, 1:2, :]
    first_f = ends[0]
    tail = ends[1]
    back_in = tail + root * beyond

    def back_body(i, bwd):
        x = LX - 1 - i
        p_spec[at_x(x), :] = factor_b * bwd
        return root * (spec[at_x(x), :] + bwd)

    lax.fori_loop(0, LX, back_body, back_in, unroll=2)

    def front_body(x, carry):
        fwd, height = carry
        fwd = spec[at_x(x), :] + root * fwd
        p_spec[at_x(x), :] = p_spec[at_x(x), :] + factor_f * jnp.where(alone, height, fwd)
        return fwd, height + fwd

    fwd, height = lax.fori_loop(0, LX, front_body, (first_f, tail), unroll=2)
    after = factor_f * jnp.where(alone, height, root * fwd) + factor_b * (root_inv * back_in)
    for part in range(N):
        at = slice(part * LANES, (part + 1) * LANES)
        for t, piece in enumerate(split_three(p_spec[part * ROWS : (part + 1) * ROWS, :])):
            y_pieces[t * MSG : t * MSG + ROWS, at] = piece
        end = jnp.concatenate([after[part * KP : (part + 1) * KP], jnp.zeros((MSG - ROWS - KP, LANES), f32)], axis=0)
        for t, piece in enumerate(split_three(end)):
            y_pieces[t * MSG + ROWS : (t + 1) * MSG, at] = piece

    def inverse(base):
        def body(n, _):
            wide = PAIR * LANES
            at = pl.ds(pl.multiple_of(base * LANES + n * wide, LANES), wide)
            first = matmul(y_pieces[...], q_tab[0, :, at])
            second = matmul(y_pieces[0 : 2 * MSG], q_tab[1, :, at])
            third = matmul(y_pieces[0:MSG], q_tab[2, :, at])
            small = second[MSG : 2 * MSG] + third + first[2 * MSG : 3 * MSG]
            result = first[0:MSG] + (first[MSG : 2 * MSG] + second[0:MSG] + small)
            for side in range(PAIR):
                o_send[base + PAIR * n + side] = result[:, side * LANES : (side + 1) * LANES]
            return 0

        lax.fori_loop(0, half // PAIR, body, 0)

    PAIR = min(2, half)
    o_x = pen_exchange(o_send, o_in, o_s, o_r)
    inverse(far_base)
    o_x[0](0, half)
    inverse(near_base)
    o_x[0](half, N - 1)
    for part in range(N):
        turned = jnp.transpose(o_send[(part + 1) % N, 0:ROWS, :])
        h_send[part] = jnp.broadcast_to(turned[0:1, :], (8, ROWS))
    h_x = pen_exchange(h_send, h_in, h_s, h_r)
    h_x[0]()
    g_x[0](S // 2, S)
    o_in[pe] = o_send[pe]
    h_in[pe] = h_send[pe]

    def velocity_part(part):
        column = jnp.transpose(jnp.broadcast_to(h_in[part, 0:1, :], (LANES, ROWS)))
        for layer in range(KP):
            k = part * KP + layer
            at = pl.ds(pl.multiple_of(k * LX, 8), LX)
            here = o_in[part, layer * LX : (layer + 1) * LX, :]
            above = o_in[part, ROWS + layer : ROWS + layer + 1, :]
            next_x = jnp.where(sub_x == LX - 1, above, pltpu.roll(here, LX - 1, 0))
            next_y = jnp.where(
                lane_x == LANES - 1, column[layer * LX : (layer + 1) * LX, :], pltpu.roll(here, LANES - 1, 1)
            )
            o_vel[pl.ds(k, LX, stride=K), :] = ax_k[at, :] - (next_x - here)
            o_vel[pl.ds(2 * LX * K + k, LX, stride=K), :] = ay_k[at, :] - (next_y - here)

    def velocity_group(base):
        def body(j, _):
            velocity_part(base + j)
            return 0

        lax.fori_loop(0, half, body, 0)

    o_x[1](half, N - 1)
    h_x[1](half, N - 1)
    velocity_group(near_base)
    o_x[1](0, half)
    h_x[1](0, half)
    velocity_group(far_base)

    late = [
        pltpu.make_async_copy(o_vel.at[pl.ds(at, block // 2)], o_vel_hbm.at[pl.ds(at, block // 2)], io_sem.at[slot])
        for slot, at in ((14, 0), (15, block // 2), (16, 2 * block), (17, 2 * block + block // 2))
    ]
    for copy in late:
        copy.start()
    g_x[1]()

    def back_home(k, _):
        o_grad[pl.ds(k, LX, stride=K), :] = g_in[pl.ds(pl.multiple_of(k * LX, 8), LX), :]
        return 0

    lax.fori_loop(0, K, back_home, 0, unroll=4)
    late += [
        pltpu.make_async_copy(o_grad.at[pl.ds(at, block // 2)], o_grad_hbm.at[pl.ds(at, block // 2)], io_sem.at[slot])
        for slot, at in ((18, 0), (19, block // 2))
    ]
    for copy in late[4:]:
        copy.start()
    for copy in stores + late:
        copy.wait()
    for copy_sends in (dens_x[2], d_x[2], c_x[2], b_x[2], g_x[2], o_x[2], h_x[2]):
        copy_sends()


def hand_over(*refs):
    count = (len(refs) - 2) // 3
    sources, targets, rooms = refs[:count], refs[count : 2 * count], refs[2 * count : 3 * count]
    in_sem, out_sem = refs[3 * count :]
    blocks = []
    for source, target, room in zip(sources, targets, rooms):
        rows = source.shape[0]
        size = min(rows, 512)
        for at in range(0, rows, size):
            part = pl.ds(at, size)
            slot = len(blocks)
            blocks.append(
                (
                    pltpu.make_async_copy(source.at[part], room.at[part], in_sem.at[slot]),
                    pltpu.make_async_copy(room.at[part], target.at[part], out_sem.at[slot]),
                )
            )
    for fetch, _ in blocks:
        fetch.start()
    for fetch, store in blocks:
        fetch.wait()
        store.start()
    for _, store in blocks:
        store.wait()


def solution(mesh):
    S, N = mesh.shape["sim"], mesh.shape["pen"]

    def shards(density, velocity, stencil_code, fractions, targets, view_start, view_sign):
        LX, K, LY = density.shape
        VIEWS = targets.shape[0]
        NX, NY = LX * S, LY * N
        tables = jnp.asarray(hartley_pieces(NY))
        lines = jnp.asarray(line_tables(NY, NX, LX, K // N))
        anywhere = pl.BlockSpec(memory_space=pl.ANY)
        vmem = pl.BlockSpec(memory_space=pltpu.VMEM)
        smem = pl.BlockSpec(memory_space=pltpu.SMEM)
        dma = pltpu.SemaphoreType.DMA
        scratch = [
            pltpu.VMEM((LX, K, LY), f32),
            pltpu.VMEM((3, LX, K, LY), f32),
            pltpu.VMEM((LX, K, LY), jnp.int32),
            pltpu.VMEM((3, LX, K, LY), f32),
            pltpu.VMEM((LX * K, LY), f32),
            pltpu.VMEM((3 * LX * K, LY), f32),
            pltpu.VMEM((LX * K, LY), f32),
            dma((20,)),
            pltpu.VMEM((3, 4, LX + 2, K, LY), f32),
            pltpu.VMEM((10, K, LY), f32),
            pltpu.VMEM((4, K, LY), f32),
            pltpu.VMEM((4, K, LY), f32),
            pltpu.VMEM((6, K, LY), f32),
            pltpu.VMEM((K * LX, LY), f32),
            pltpu.VMEM((K * LX, LY), f32),
            pltpu.VMEM((K * LX, LY), f32),
            pltpu.VMEM((NX, LY), f32),
            pltpu.VMEM((N, MSG, LY), f32),
            pltpu.VMEM((N, MSG, LY), f32),
            pltpu.VMEM((2, 2 * MSG, NY // 2 + LANES), bf16),
            pltpu.VMEM((3, NY, NY), bf16),
            pltpu.VMEM((N * 128, LANES), f32),
            pltpu.VMEM((N, 8, LANES), f32),
            pltpu.VMEM((S, 2, LANES), f32),
            pltpu.VMEM((S, 2, LANES), f32),
            pltpu.VMEM((S, 2, LANES), f32),
            pltpu.VMEM((S, 2, LANES), f32),
            pltpu.VMEM((2, S, LANES), f32),
            pltpu.VMEM((N * 128, LANES), f32),
            pltpu.VMEM((3 * MSG, NY), bf16),
            pltpu.VMEM((N, MSG, LY), f32),
            pltpu.VMEM((N, MSG, LY), f32),
            pltpu.VMEM((N, 8, LY), f32),
            pltpu.VMEM((N, 8, LY), f32),
            pltpu.VMEM((NX, LY), f32),
            pltpu.VMEM((NX, LY), f32),
            pltpu.VMEM((NX, LY), f32),
            pltpu.VMEM((4, VIEWS, LY), f32),
            pltpu.VMEM((6 * VIEWS, 3 * LY), bf16),
            pltpu.VMEM((NX, 3 * LY), f32),
            pltpu.VMEM((NX, LY), f32),
            pltpu.VMEM((K * LX, LY), f32),
            dma((8,)), dma((8,)),
            dma((S,)), dma((S,)),
            dma((N,)), dma((N,)),
            dma((S,)), dma((S,)),
            dma((S,)), dma((S,)),
            dma((N,)), dma((N,)),
            dma((S,)), dma((S,)),
            dma((N,)), dma((N,)),
            dma((3,)),
        ]
        density_new, velocity_new, images, gradient = pl.pallas_call(
            functools.partial(step_kernel, (S, N, LX, K, VIEWS)),
            out_shape=(
                jax.ShapeDtypeStruct((LX * K, LY), f32),
                jax.ShapeDtypeStruct((3 * LX * K, LY), f32),
                jax.ShapeDtypeStruct(targets.shape, f32),
                jax.ShapeDtypeStruct((LX * K, LY), f32),
            ),
            in_specs=[anywhere] * 4 + [vmem, smem, smem, anywhere, vmem],
            out_specs=(anywhere, anywhere, vmem, anywhere),
            scratch_shapes=scratch,
            compiler_params=pltpu.CompilerParams(
                collective_id=0, has_side_effects=True, vmem_limit_bytes=60 * 1024 * 1024
            ),
        )(density, velocity, stencil_code, fractions, targets, view_start, view_sign, tables, lines)
        results = (density_new, velocity_new, images, gradient)
        shapes = tuple(jax.ShapeDtypeStruct(value.shape, value.dtype) for value in results)
        density_new, velocity_new, images, gradient = pl.pallas_call(
            hand_over,
            out_shape=shapes,
            in_specs=[anywhere] * 4,
            out_specs=(anywhere,) * 4,
            scratch_shapes=[pltpu.VMEM(shape.shape, f32) for shape in shapes] + [dma((32,)), dma((32,))],
            compiler_params=pltpu.CompilerParams(vmem_limit_bytes=60 * 1024 * 1024),
        )(*results)
        return (
            density_new.reshape(LX, K, LY),
            velocity_new.reshape(3, LX, K, LY),
            images,
            gradient.reshape(LX, K, LY),
        )

    return jax.shard_map(
        shards,
        mesh=mesh,
        in_specs=(
            P("sim", None, "pen"),
            P(None, "sim", None, "pen"),
            P("sim", None, "pen"),
            P(None, "sim", None, "pen"),
            P(None, "sim", "pen"),
            P(),
            P(),
        ),
        out_specs=(
            P("sim", None, "pen"),
            P(None, "sim", None, "pen"),
            P(None, "sim", "pen"),
            P("sim", None, "pen"),
        ),
        check_vma=False,
    )
```

```python
import functools

import jax
import jax.numpy as jnp
import numpy as np
from jax import lax
from jax.experimental import pallas as pl
from jax.experimental.pallas import tpu as pltpu
from jax.sharding import PartitionSpec as P

STEPS = 256
ABSORB = 2.0 / STEPS
LANES = 128
SEGMENTS = 8
MSG = 144
f32 = jnp.float32
bf16 = jnp.bfloat16


def hartley_pieces(length):
    index = np.arange(length)
    angles = (np.outer(index, index) % length) * (2.0 * np.pi / length)
    table = (np.cos(angles) + np.sin(angles)) / np.sqrt(length)
    pieces = []
    for _ in range(3):
        piece = table.astype(jnp.bfloat16)
        pieces.append(piece)
        table = table - piece.astype(np.float64)
    return np.stack(pieces)


def line_tables(length_y, length_x, local_x, layers):
    eig = 4.0 * np.sin(np.pi * np.arange(length_y) / length_y) ** 2
    half = eig / 2.0
    root = 1.0 / (1.0 + half + np.sqrt(half * (half + 2.0)))
    gap = 1.0 / root - root
    gap[0] = 1.0
    forward = -1.0 / gap
    backward = -1.0 / gap
    forward[0] = 1.0
    backward[0] = 0.0
    block = root**local_x
    closing = 1.0 - root**length_x
    closing[0] = 1.0
    closing = 1.0 / closing
    closing[0] = 0.0
    rows = np.stack([root, 1.0 / root, forward, backward, block, closing])
    rows = rows.reshape(6, length_y // LANES, 1, LANES)
    return np.repeat(rows, layers, axis=2).reshape(6, -1, LANES).astype(np.float32)


def split_two(values):
    high = values.astype(bf16)
    low = (values - high.astype(f32)).astype(bf16)
    return high, low


def split_three(values):
    high = values.astype(bf16)
    rest = values - high.astype(f32)
    mid = rest.astype(bf16)
    low = (rest - mid.astype(f32)).astype(bf16)
    return high, mid, low


def iota(shape, dim):
    return lax.broadcasted_iota(jnp.int32, shape, dim)


def matmul(a, b):
    return jnp.dot(a, b, preferred_element_type=f32)


def step_kernel(
    sizes,
    dens_hbm, vel_hbm, code_hbm, frac_hbm, targ, vstart, vsign, tables_hbm, lines, q_first,
    o_dens_hbm, o_vel_hbm, o_img, o_grad_hbm,
    dens, vel, code, frac, o_dens, o_vel, o_grad, io_sem,
    ext, pack, xlo, xhi, pin, dens_k, ax_k, ay_k,
    rays, d_send, d_in, x_pieces, q_tab, spec, spec_end,
    c_send, c_in, c_out, c_ret, ends, p_spec, y_pieces, o_send, o_in, h_send, h_in, h_columns,
    prefix, w_light, v_light, gathered, rhs, sums, g_send, g_in,
    halo_s, halo_r, dens_s, dens_r, d_s, d_r, c_s, c_r, b_s, b_r, o_s, o_r, g_s, g_r, h_s, h_r, tab_sem,
):
    S, N, LX, K, VIEWS = sizes
    KP = K // N
    NX, NY = S * LX, N * LANES
    ROWS = KP * LX
    SENT = ROWS + 8
    SEG = NX // SEGMENTS
    me = lax.axis_index("sim")
    pe = lax.axis_index("pen")

    def simp(off):
        return lax.rem(me + off + S, S)

    def penp(off):
        return lax.rem(pe + off + N, N)

    def balanced(i, count):
        odd = lax.rem(i, 2)
        half = (i + 1) // 2
        return odd * half + (1 - odd) * (count - half)

    parts = LX // 2
    fields_in = [pltpu.make_async_copy(dens_hbm.at[pl.ds(h * parts, parts)], dens.at[pl.ds(h * parts, parts)], io_sem.at[h]) for h in range(2)]
    fields_in += [
        pltpu.make_async_copy(vel_hbm.at[c, pl.ds(h * parts, parts)], vel.at[c, pl.ds(h * parts, parts)], io_sem.at[2 + 2 * c + h])
        for c in range(3)
        for h in range(2)
    ]
    weights_in = [pltpu.make_async_copy(code_hbm, code, io_sem.at[8])]
    weights_in += [pltpu.make_async_copy(frac_hbm.at[c], frac.at[c], io_sem.at[9 + c]) for c in range(3)]
    for copy in fields_in + weights_in:
        copy.start()
    table_copies = [pltpu.make_async_copy(tables_hbm.at[t], q_tab.at[t], tab_sem.at[t]) for t in range(3)]
    for copy in table_copies:
        copy.start()

    barrier = pltpu.get_barrier_semaphore()

    def greet_sim(off, _):
        pl.semaphore_signal(barrier, inc=1, device_id={"sim": simp(off), "pen": pe}, device_id_type=pl.DeviceIdType.MESH)
        return 0

    def greet_pen(off, _):
        pl.semaphore_signal(barrier, inc=1, device_id={"sim": me, "pen": penp(off)}, device_id_type=pl.DeviceIdType.MESH)
        return 0

    lax.fori_loop(1, S, greet_sim, 0)
    lax.fori_loop(1, N, greet_pen, 0)
    corners = ((-1, -1), (-1, 1), (1, -1), (1, 1))
    for dx, dy in corners:
        pl.semaphore_signal(barrier, inc=1, device_id={"sim": simp(dx), "pen": penp(dy)}, device_id_type=pl.DeviceIdType.MESH)

    for copy in fields_in:
        copy.wait()

    lane = iota((K, LANES), 1)

    def source(field, x):
        return dens[x] if field == 0 else vel[field - 1, x]

    def pack_body(x, carry):
        first, last = carry
        for field in range(4):
            cells = source(field, x)
            spot = field * LX + x
            here = lane == spot
            first = jnp.where(here, pltpu.roll(cells, spot, 1), first)
            last = jnp.where(here, pltpu.roll(cells, lax.rem(spot + 1, LANES), 1), last)
        return first, last

    nothing = jnp.zeros((K, LANES), f32)
    first, last = lax.fori_loop(0, LX, pack_body, (nothing, nothing), unroll=4)
    pack[0] = first
    pack[1] = last
    for field in range(4):
        pack[2 + field] = source(field, 0)
        pack[6 + field] = source(field, LX - 1)

    pl.semaphore_wait(barrier, (S - 1) + (N - 1) + 4)

    def remote(src, dst, s_sem, r_sem, sim, pen):
        return pltpu.make_async_remote_copy(
            src_ref=src, dst_ref=dst, send_sem=s_sem, recv_sem=r_sem,
            device_id={"sim": sim, "pen": pen}, device_id_type=pl.DeviceIdType.MESH,
        )

    halo = [
        remote(pack.at[pl.ds(6, 4)], xlo, halo_s.at[0], halo_r.at[0], simp(1), pe),
        remote(pack.at[pl.ds(2, 4)], xhi, halo_s.at[1], halo_r.at[1], simp(-1), pe),
    ]
    for side in range(2):
        for dx in (-1, 0, 1):
            slot = side * 3 + 1 + dx
            halo.append(
                remote(
                    pack.at[1 - side], pin.at[slot], halo_s.at[2 + slot], halo_r.at[2 + slot],
                    simp(-dx), penp(1 if side == 0 else -1),
                )
            )
    for copy in halo:
        copy.start()

    def spread_body(x, _):
        for field in range(4):
            cells = source(field, x)
            ext[0, field, x + 1] = pltpu.roll(cells, 1, 1)
            ext[1, field, x + 1] = cells
            ext[2, field, x + 1] = pltpu.roll(cells, LANES - 1, 1)
        return 0

    lax.fori_loop(0, LX, spread_body, 0, unroll=4)
    for copy in halo:
        copy.wait()

    is_first = lane == 0
    is_last = lane == LANES - 1

    def fix_body(x, _):
        for field in range(4):
            spot = field * LX + x
            left = pltpu.roll(pin[1], LANES - spot, 1)
            right = pltpu.roll(pin[4], LANES - 1 - spot, 1)
            ext[0, field, x + 1] = jnp.where(is_first, left, ext[0, field, x + 1])
            ext[2, field, x + 1] = jnp.where(is_last, right, ext[2, field, x + 1])
        return 0

    lax.fori_loop(0, LX, fix_body, 0, unroll=8)
    for row, rows, slot, at in ((0, xlo, 0, LX - 1), (LX + 1, xhi, 2, 0)):
        for field in range(4):
            spot = field * LX + at
            cells = rows[field]
            left = pltpu.roll(pin[slot], (LANES - spot) % LANES, 1)
            right = pltpu.roll(pin[3 + slot], LANES - 1 - spot, 1)
            ext[0, field, row] = jnp.where(is_first, left, pltpu.roll(cells, 1, 1))
            ext[1, field, row] = cells
            ext[2, field, row] = jnp.where(is_last, right, pltpu.roll(cells, LANES - 1, 1))

    for copy in weights_in:
        copy.wait()

    def weights(bit, fraction):
        rest = 1.0 - fraction
        on = bit == 1
        return (jnp.where(on, rest, 0.0), jnp.where(on, fraction, rest), jnp.where(on, 0.0, fraction))

    def advect_body(x, _):
        codes = code[x]
        wx = weights(codes & 1, frac[0, x])
        wz = weights((codes >> 1) & 1, frac[1, x])
        wy = weights((codes >> 2) & 1, frac[2, x])
        totals = [None] * 4
        for slot, shift in ((1, 0), (0, -1), (2, 1)):
            if shift == 0:
                rx, ry = wx, wy
            else:
                amount = shift % K
                rx = [pltpu.roll(w, amount, 0) for w in wx]
                ry = [pltpu.roll(w, amount, 0) for w in wy]
            for field in range(4):
                term = None
                for sy in range(3):
                    part = (
                        rx[0] * ext[sy, field, x]
                        + rx[1] * ext[sy, field, x + 1]
                        + rx[2] * ext[sy, field, x + 2]
                    )
                    term = ry[sy] * part if term is None else term + ry[sy] * part
                if shift != 0:
                    term = pltpu.roll(term, (-shift) % K, 0)
                term = wz[slot] * term
                totals[field] = term if totals[field] is None else totals[field] + term
        o_dens[pl.ds(pl.multiple_of(x * K, 8), K), :] = totals[0]
        o_vel[pl.ds(pl.multiple_of(LX * K + x * K, 8), K), :] = totals[2]
        dens_k[pl.ds(x, K, stride=LX), :] = totals[0]
        ax_k[pl.ds(x, K, stride=LX), :] = totals[1]
        ay_k[pl.ds(x, K, stride=LX), :] = totals[3]
        return 0

    lax.fori_loop(0, LX, advect_body, 0)
    block = LX * K
    stores = [
        pltpu.make_async_copy(o_dens, o_dens_hbm, io_sem.at[12]),
        pltpu.make_async_copy(o_vel.at[pl.ds(block, block)], o_vel_hbm.at[pl.ds(block, block)], io_sem.at[13]),
    ]
    for copy in stores:
        copy.start()

    def sim_exchange(src, src_rows, dst, s_sem, r_sem):
        def descriptor(peer, start_at):
            if src_rows:
                a = src.at[pl.ds(pl.multiple_of(peer * src_rows, 8), src_rows)]
                b = dst.at[pl.ds(pl.multiple_of(start_at * src_rows, 8), src_rows)]
            else:
                a, b = src.at[peer], dst.at[start_at]
            return remote(a, b, s_sem.at[peer], r_sem.at[start_at], peer, pe)

        def start(first=1, end=S):
            def body(i, _):
                descriptor(simp(balanced(i, S)), me).start()
                return 0

            lax.fori_loop(first, end, body, 0)

        def wait_recv():
            def body(off, _):
                peer = simp(off)
                descriptor(peer, peer).wait_recv()
                return 0

            lax.fori_loop(1, S, body, 0)

        def wait_send():
            def body(off, _):
                descriptor(simp(off), me).wait_send()
                return 0

            lax.fori_loop(1, S, body, 0)

        def wait_one(i):
            peer = simp(balanced(i, S))
            descriptor(peer, peer).wait_recv()

        return start, wait_recv, wait_send, wait_one

    half = N // 2
    near_base = lax.div(pe, half) * half
    far_base = half - near_base

    def pen_peer(i):
        near = near_base + lax.rem(pe - near_base + 1 + i, half)
        return jnp.where(i < half, far_base + i, near)

    def pen_exchange(src, dst, s_sem, r_sem):
        def descriptor(peer, start_at):
            return remote(src.at[peer], dst.at[start_at], s_sem.at[peer], r_sem.at[start_at], me, peer)

        def loop(method, swap):
            def run(first=0, end=N - 1):
                def body(i, _):
                    peer = pen_peer(i)
                    getattr(descriptor(peer, peer if swap else pe), method)()
                    return 0

                lax.fori_loop(first, end, body, 0)

            return run

        return loop("start", False), loop("wait_recv", True), loop("wait_send", False)

    dens_x = sim_exchange(dens_k, LX, rays, dens_s, dens_r)
    early = S // 4
    dens_x[0](1, early)
    mine = pl.ds(pl.multiple_of(me * LX, 8), LX)
    rays[mine, :] = dens_k[mine, :]

    sub_x = iota((LX, LANES), 0)
    lane_x = iota((LX, LANES), 1)

    def div_part(part):
        base = part * ROWS
        ends = []
        for layer in range(KP):
            at = pl.ds(pl.multiple_of(base + layer * LX, 8), LX)
            ax = ax_k[at, :]
            ay = ay_k[at, :]
            before_x = jnp.where(sub_x == 0, 0.0, pltpu.roll(ax, 1, 0))
            before_y = jnp.where(lane_x == 0, 0.0, pltpu.roll(ay, 1, 1))
            d_send[part, layer * LX : (layer + 1) * LX, :] = (ax - before_x) + (ay - before_y)
            ends.append(-ax[LX - 1 : LX, :])
        turned = jnp.transpose(ay_k[pl.ds(pl.multiple_of(base, 8), ROWS), :])
        ends.append(turned[LANES - 1 : LANES, :])
        d_send[part, ROWS:SENT, :] = jnp.concatenate(ends + [jnp.zeros((7 - KP, LANES), f32)], axis=0)

    d_x = pen_exchange(d_send, d_in, d_s, d_r)

    def div_send(i, _):
        div_part(pen_peer(i))
        d_x[0](i, i + 1)
        return 0

    lax.fori_loop(0, N - 1, div_send, 0)
    div_part(pe)
    dens_x[0](early, S)
    d_in[pe] = d_send[pe]
    for copy in table_copies:
        copy.wait()

    WIDE = half * LANES

    def stage(group, at, cells, end):
        for t, piece in enumerate(split_two(cells)):
            x_pieces[group, t * MSG : t * MSG + ROWS, at] = piece
        for t, piece in enumerate(split_two(end)):
            x_pieces[group, t * MSG + ROWS : (t + 1) * MSG, at] = piece

    def stage_group(group, base):
        for j in range(half):
            cells = d_in[base + j, 0:ROWS, :]
            end = jnp.concatenate([d_in[base + j, ROWS : ROWS + KP, :], jnp.zeros((MSG - ROWS - KP, LANES), f32)], axis=0)
            stage(group, slice(j * LANES, (j + 1) * LANES), cells, end)

    def transform(group, table, rows, columns):
        wide = 2 * LANES

        def body(n, _):
            at = pl.ds(pl.multiple_of(n * wide, wide), wide)
            both = matmul(x_pieces[group, :, columns], table[0, rows, at])
            high = matmul(x_pieces[group, 0:MSG, columns], table[1, rows, at])
            result = both[0:MSG] + (both[MSG : 2 * MSG] + high)
            for side in range(2):
                values = result[:, side * LANES : (side + 1) * LANES]
                line = pl.ds(pl.multiple_of((2 * n + side) * ROWS, 8), ROWS)
                if group == 0:
                    spec[line, :] = values[0:ROWS]
                    spec_end[2 * n + side] = values[ROWS : ROWS + 8]
                else:
                    spec[line, :] = spec[line, :] + values[0:ROWS]
                    spec_end[2 * n + side] = spec_end[2 * n + side] + values[ROWS : ROWS + 8]
            return 0

        lax.fori_loop(0, NY // wide, body, 0)

    d_x[1](half, N - 1)
    stage_group(0, near_base)
    transform(0, q_tab, pl.ds(pl.multiple_of(near_base * LANES, LANES), WIDE), slice(0, WIDE))
    d_x[1](0, half)
    stage_group(1, far_base)
    ahead = jnp.concatenate(
        [d_in[part, ROWS + KP : ROWS + KP + 1, :] for part in range(N)] + [jnp.zeros((LANES - N, ROWS), f32)], axis=0
    )
    stage(1, slice(WIDE, WIDE + LANES), -jnp.transpose(ahead), jnp.zeros((MSG - ROWS, LANES), f32))
    transform(1, q_tab, pl.ds(pl.multiple_of(far_base * LANES, LANES), WIDE), slice(0, WIDE))
    transform(1, q_first, slice(0, LANES), slice(WIDE, WIDE + LANES))

    LINES = N * KP
    root = lines[0]
    root_inv = lines[1]
    beyond = jnp.concatenate([spec_end[part, 0:KP, :] for part in range(N)], axis=0)
    flat = jnp.zeros((LINES, LANES), f32)

    def at_x(x):
        return pl.ds(x, LINES, stride=LX)

    def ends_body(i, carry):
        fwd, bwd, acc = carry
        fwd = spec[at_x(i), :] + root * fwd
        acc = acc + fwd
        bwd = root * (spec[at_x(LX - 1 - i), :] + bwd)
        return fwd, bwd, acc

    fwd, bwd, acc = lax.fori_loop(0, LX, ends_body, (flat, root * beyond, flat), unroll=4)
    fwd = fwd + root_inv * beyond

    alone = jnp.logical_and(iota((LINES, LANES), 1) == 0, iota((LINES, LANES), 0) < KP)
    bwd = jnp.where(alone, acc, bwd)
    for line in range(LINES):
        c_send[line, 0:1, :] = fwd[line : line + 1]
        c_send[line, 1:2, :] = bwd[line : line + 1]
    c_x = sim_exchange(c_send, 0, c_in, c_s, c_r)
    c_x[0]()
    c_in[me] = c_send[me]

    dens_x[1]()

    def strided(x):
        return pl.ds(x, SEGMENTS, stride=SEG)

    def chain(x):
        return pl.ds(pl.multiple_of(x * SEGMENTS, SEGMENTS), SEGMENTS)

    seg0 = jnp.zeros((SEGMENTS, LANES), f32)

    def scan_body(i, carry):
        depth, down, up = carry
        back = SEG - 1 - i
        glow = ABSORB * rays[strided(i), :]
        prefix[chain(i), :] = depth
        depth = depth + glow
        down = glow + jnp.exp(-glow) * down
        v_light[chain(i), :] = down
        glow_b = ABSORB * rays[strided(back), :]
        up = glow_b + jnp.exp(-glow_b) * up
        w_light[chain(back), :] = up
        return depth, down, up

    seg_depth, seg_down, seg_up = lax.fori_loop(0, SEG, scan_body, (seg0, seg0, seg0), unroll=4)
    seg_pass = jnp.exp(-seg_depth)
    one = jnp.zeros((1, LANES), f32)
    total_depth, run_down, run_up = one, one, one
    starts = []
    for g in range(SEGMENTS):
        starts.append(total_depth)
        total_depth = total_depth + seg_depth[g : g + 1, :]
        run_down = seg_down[g : g + 1, :] + seg_pass[g : g + 1, :] * run_down
        h = SEGMENTS - 1 - g
        run_up = seg_up[h : h + 1, :] + seg_pass[h : h + 1, :] * run_up
    total_pass = jnp.exp(-total_depth)
    closing = 1.0 / (1.0 - total_pass)
    run_down = run_down * closing
    run_up = run_up * closing
    downs, ups = [], []
    for g in range(SEGMENTS):
        downs.append(run_down)
        run_down = seg_down[g : g + 1, :] + seg_pass[g : g + 1, :] * run_down
        h = SEGMENTS - 1 - g
        ups.append(run_up)
        run_up = seg_up[h : h + 1, :] + seg_pass[h : h + 1, :] * run_up
    start_depth = jnp.concatenate(starts, axis=0)
    down_in = jnp.concatenate(downs, axis=0)
    up_in = jnp.concatenate(ups[::-1], axis=0)

    def finish_body(i, _):
        glow = ABSORB * rays[strided(i), :]
        depth = prefix[chain(i), :]
        v_light[chain(i), :] = v_light[chain(i), :] + jnp.exp(-(depth + glow)) * down_in
        w_light[chain(i), :] = w_light[chain(i), :] + jnp.exp(depth - seg_depth) * up_in
        prefix[chain(i), :] = depth + start_depth
        return 0

    lax.fori_loop(0, SEG, finish_body, 0, unroll=4)

    c_x[1]()
    power = lines[4, pl.ds(me, 1), :]
    close = lines[5, pl.ds(me, 1), :]
    lone = jnp.logical_and(iota((1, LANES), 1) == 0, me < KP)

    def around_body(i, carry):
        a, b = carry
        a = c_in[i, 0:1, :] + power * a
        b = c_in[S - 1 - i, 1:2, :] + power * b
        return a, b

    a, b = lax.fori_loop(0, S, around_body, (one, one), unroll=8)

    def carry_body(i, carry):
        a, b, total = carry
        j = S - 1 - i
        c_out[i, 0:1, :] = a
        c_out[j, 1:2, :] = b
        total = total + (c_in[i, 1:2, :] + LX * a)
        return c_in[i, 0:1, :] + power * a, c_in[j, 1:2, :] + power * b, total

    _, _, total = lax.fori_loop(0, S, carry_body, (a * close, b * close, one), unroll=8)
    mean = total * (1.0 / NX)

    def lone_body(i, offset):
        slope = c_out[i, 0:1, :] - mean
        c_out[i, 0:1, :] = jnp.where(lone, slope, c_out[i, 0:1, :])
        c_out[i, 1:2, :] = jnp.where(lone, offset, c_out[i, 1:2, :])
        return offset + (c_in[i, 1:2, :] + LX * slope)

    lax.fori_loop(0, S, lone_body, one, unroll=8)
    b_x = sim_exchange(c_out, 0, c_ret, b_s, b_r)
    b_x[0]()
    c_ret[me] = c_out[me]

    sub_v = iota((VIEWS, LANES), 0)
    lane_m = iota((1, 6 * VIEWS), 1)
    view_m = lax.rem(lane_m, VIEWS)

    def where_is(x):
        return lax.rem(x, SEG) * SEGMENTS + lax.div(x, SEG)

    def view_body(v, carry):
        ups_v, start_m, up_m = carry
        x0 = vstart[v]
        up = vsign[v] == 1
        far = jnp.where(up, x0 + STEPS, x0 - STEPS)
        wraps = jnp.logical_or(far >= NX, far < 0)
        xe = jnp.where(far >= NX, far - NX, jnp.where(far < 0, far + NX, far))
        out = []
        for x in (x0, xe):
            at = pl.ds(where_is(x), 1)
            depth = prefix[at, :]
            depth = jnp.where(up, depth, -(depth + ABSORB * rays[pl.ds(x, 1), :]))
            out.append((depth, jnp.where(up, w_light[at, :], v_light[at, :])))
        gathered[0, pl.ds(v, 1), :] = out[0][0]
        gathered[1, pl.ds(v, 1), :] = out[0][1]
        gathered[2, pl.ds(v, 1), :] = out[1][0] + jnp.where(wraps, total_depth, 0.0)
        gathered[3, pl.ds(v, 1), :] = out[1][1]
        flag = vsign[v]
        return (
            jnp.where(sub_v == v, flag, ups_v),
            jnp.where(view_m == v, x0, start_m),
            jnp.where(view_m == v, flag, up_m),
        )

    none_m = jnp.zeros((1, 6 * VIEWS), jnp.int32)
    ups_v, start_m, up_m = lax.fori_loop(0, VIEWS, view_body, (jnp.zeros((VIEWS, LANES), jnp.int32), none_m, none_m))
    entry, light0, leave, light1 = gathered[0], gathered[1], gathered[2], gathered[3]
    seen_through = jnp.exp(entry - leave) * light1
    picture = light0 - seen_through
    o_img[:, 0, :] = picture
    pull = (STEPS * ABSORB) * (picture - targ[:, 0, :])
    coef = pull * jnp.exp(entry)
    alpha = jnp.where(ups_v == 1, coef, 0.0)
    gamma = jnp.where(ups_v == 1, 0.0, coef)
    beta = pull * seen_through
    for slot, value in enumerate((alpha, gamma, beta)):
        wrapped = beta if slot == 2 else value * total_pass
        both = jnp.concatenate([value, wrapped], axis=0)
        for t, piece in enumerate(split_three(both)):
            rhs[t * 2 * VIEWS : (t + 1) * 2 * VIEWS, slot * LANES : (slot + 1) * LANES] = piece

    kind = lax.rem(lax.div(lane_m, VIEWS), 2) == 1
    tile = 256

    def window_body(n, _):
        row = n * tile + iota((tile, 6 * VIEWS), 0)
        x = lax.rem(row, SEGMENTS) * SEG + lax.div(row, SEGMENTS)
        delta = jnp.where(up_m == 1, x - start_m, start_m - x)
        back = delta < 0
        inside = jnp.where(back, delta + NX, delta) < STEPS
        chosen = jnp.logical_and(inside, jnp.logical_xor(back, jnp.logical_not(kind)))
        mask = jnp.where(chosen, 1.0, 0.0).astype(bf16)
        sums[pl.ds(pl.multiple_of(n * tile, tile), tile), :] = matmul(mask, rhs[...])
        return 0

    lax.fori_loop(0, NX // tile, window_body, 0)

    def grad_body(i, _):
        glow = ABSORB * rays[strided(i), :]
        depth = prefix[chain(i), :]
        terms = sums[chain(i), :]
        g_send[strided(i), :] = (
            jnp.exp(-depth) * (1.0 - w_light[chain(i), :] + glow) * terms[:, 0:LANES]
            + jnp.exp(depth + glow) * (1.0 - v_light[chain(i), :] + glow) * terms[:, LANES : 2 * LANES]
            + terms[:, 2 * LANES : 3 * LANES]
        )
        return 0

    lax.fori_loop(0, SEG, grad_body, 0, unroll=4)
    g_x = sim_exchange(g_send, LX, g_in, g_s, g_r)
    g_x[0](1, S // 2)
    g_in[mine, :] = g_send[mine, :]

    b_x[1]()
    factor_f = lines[2]
    factor_b = lines[3]
    for line in range(LINES):
        ends[0, line : line + 1, :] = c_ret[line, 0:1, :]
        ends[1, line : line + 1, :] = c_ret[line, 1:2, :]
    first_f = ends[0]
    tail = ends[1]
    back_in = tail + root * beyond

    def back_body(i, bwd):
        x = LX - 1 - i
        p_spec[at_x(x), :] = factor_b * bwd
        return root * (spec[at_x(x), :] + bwd)

    lax.fori_loop(0, LX, back_body, back_in, unroll=4)

    def front_body(x, carry):
        fwd, height = carry
        fwd = spec[at_x(x), :] + root * fwd
        p_spec[at_x(x), :] = p_spec[at_x(x), :] + factor_f * jnp.where(alone, height, fwd)
        return fwd, height + fwd

    fwd, height = lax.fori_loop(0, LX, front_body, (first_f, tail), unroll=4)
    after = factor_f * jnp.where(alone, height, root * fwd) + factor_b * (root_inv * back_in)
    for part in range(N):
        at = slice(part * LANES, (part + 1) * LANES)
        for t, piece in enumerate(split_three(p_spec[part * ROWS : (part + 1) * ROWS, :])):
            y_pieces[t * MSG : t * MSG + ROWS, at] = piece
        end = jnp.concatenate([after[part * KP : (part + 1) * KP], jnp.zeros((MSG - ROWS - KP, LANES), f32)], axis=0)
        for t, piece in enumerate(split_three(end)):
            y_pieces[t * MSG + ROWS : (t + 1) * MSG, at] = piece

    def inverse(base, far):
        def body(n, _):
            wide = PAIR * LANES
            at = pl.ds(pl.multiple_of(base * LANES + n * wide, LANES), wide)
            first = matmul(y_pieces[...], q_tab[0, :, at])
            second = matmul(y_pieces[0 : 2 * MSG], q_tab[1, :, at])
            third = matmul(y_pieces[0:MSG], q_tab[2, :, at])
            small = second[MSG : 2 * MSG] + third + first[2 * MSG : 3 * MSG]
            result = first[0:MSG] + (first[MSG : 2 * MSG] + second[0:MSG] + small)
            for side in range(PAIR):
                o_send[base + PAIR * n + side] = result[0:SENT, side * LANES : (side + 1) * LANES]
            if far:
                o_x[0](PAIR * n, PAIR * (n + 1))
            return 0

        lax.fori_loop(0, half // PAIR, body, 0)

    PAIR = min(2, half)
    o_x = pen_exchange(o_send, o_in, o_s, o_r)
    inverse(far_base, True)
    inverse(near_base, False)
    o_x[0](half, N - 1)
    for part in range(N):
        turned = jnp.transpose(o_send[(part + 1) % N, 0:ROWS, :])
        h_send[part] = jnp.broadcast_to(turned[0:1, :], (8, ROWS))
    h_x = pen_exchange(h_send, h_in, h_s, h_r)
    h_x[0]()
    g_x[0](S // 2, S)
    o_in[pe] = o_send[pe]
    h_in[pe] = h_send[pe]

    def velocity_part(part):
        column = pltpu.roll(h_columns[...], LANES - 1 - part, 1)
        for layer in range(KP):
            k = part * KP + layer
            at = pl.ds(pl.multiple_of(k * LX, 8), LX)
            here = o_in[part, layer * LX : (layer + 1) * LX, :]
            above = o_in[part, ROWS + layer : ROWS + layer + 1, :]
            next_x = jnp.where(sub_x == LX - 1, above, pltpu.roll(here, LX - 1, 0))
            next_y = jnp.where(
                lane_x == LANES - 1, column[layer * LX : (layer + 1) * LX, :], pltpu.roll(here, LANES - 1, 1)
            )
            o_vel[pl.ds(k, LX, stride=K), :] = ax_k[at, :] - (next_x - here)
            o_vel[pl.ds(2 * LX * K + k, LX, stride=K), :] = ay_k[at, :] - (next_y - here)

    def velocity_group(base):
        def body(j, _):
            velocity_part(base + j)
            return 0

        lax.fori_loop(0, half, body, 0)

    h_x[1]()
    heads = jnp.concatenate([h_in[part, 0:1, :] for part in range(N)] + [jnp.zeros((LANES - N, ROWS), f32)], axis=0)
    h_columns[...] = jnp.transpose(heads)
    o_x[1](half, N - 1)
    velocity_group(near_base)

    def back_home(k):
        o_grad[pl.ds(k, LX, stride=K), :] = g_in[pl.ds(pl.multiple_of(k * LX, 8), LX), :]

    def bring_home(i, _):
        g_x[3](i)
        back_home(simp(balanced(i, S)))
        return 0

    back_home(me)
    lax.fori_loop(1, S // 2, bring_home, 0)

    def far_velocity(i, _):
        o_x[1](i, i + 1)
        velocity_part(far_base + i)
        return 0

    lax.fori_loop(0, half, far_velocity, 0)

    late = [
        pltpu.make_async_copy(o_vel.at[pl.ds(at, block // 2)], o_vel_hbm.at[pl.ds(at, block // 2)], io_sem.at[slot])
        for slot, at in ((14, 0), (15, block // 2), (16, 2 * block), (17, 2 * block + block // 2))
    ]
    for copy in late:
        copy.start()
    lax.fori_loop(S // 2, S, bring_home, 0)
    late += [
        pltpu.make_async_copy(o_grad.at[pl.ds(at, block // 2)], o_grad_hbm.at[pl.ds(at, block // 2)], io_sem.at[slot])
        for slot, at in ((18, 0), (19, block // 2))
    ]
    for copy in late[4:]:
        copy.start()
    for copy in stores + late:
        copy.wait()
    for copy_sends in (dens_x[2], d_x[2], c_x[2], b_x[2], g_x[2], o_x[2], h_x[2]):
        copy_sends()


def hand_over(*refs):
    count = (len(refs) - 2) // 3
    sources, targets, rooms = refs[:count], refs[count : 2 * count], refs[2 * count : 3 * count]
    in_sem, out_sem = refs[3 * count :]
    blocks = []
    for source, target, room in zip(sources, targets, rooms):
        rows = source.shape[0]
        size = min(rows, 512)
        for at in range(0, rows, size):
            part = pl.ds(at, size)
            slot = len(blocks)
            blocks.append(
                (
                    pltpu.make_async_copy(source.at[part], room.at[part], in_sem.at[slot]),
                    pltpu.make_async_copy(room.at[part], target.at[part], out_sem.at[slot]),
                )
            )
    for fetch, _ in blocks:
        fetch.start()
    for fetch, store in blocks:
        fetch.wait()
        store.start()
    for _, store in blocks:
        store.wait()


def solution(mesh):
    S, N = mesh.shape["sim"], mesh.shape["pen"]

    def shards(density, velocity, stencil_code, fractions, targets, view_start, view_sign):
        LX, K, LY = density.shape
        VIEWS = targets.shape[0]
        NX, NY = LX * S, LY * N
        pieces = hartley_pieces(NY)
        tables = jnp.asarray(pieces)
        chosen = pieces[0:2, (np.arange(1, N + 1) * LY) % NY]
        firsts = jnp.asarray(np.concatenate([chosen, np.zeros((2, LANES - N, NY), chosen.dtype)], axis=1))
        lines = jnp.asarray(line_tables(NY, NX, LX, K // N))
        anywhere = pl.BlockSpec(memory_space=pl.ANY)
        vmem = pl.BlockSpec(memory_space=pltpu.VMEM)
        smem = pl.BlockSpec(memory_space=pltpu.SMEM)
        dma = pltpu.SemaphoreType.DMA
        scratch = [
            pltpu.VMEM((LX, K, LY), f32),
            pltpu.VMEM((3, LX, K, LY), f32),
            pltpu.VMEM((LX, K, LY), jnp.int32),
            pltpu.VMEM((3, LX, K, LY), f32),
            pltpu.VMEM((LX * K, LY), f32),
            pltpu.VMEM((3 * LX * K, LY), f32),
            pltpu.VMEM((LX * K, LY), f32),
            dma((20,)),
            pltpu.VMEM((3, 4, LX + 2, K, LY), f32),
            pltpu.VMEM((10, K, LY), f32),
            pltpu.VMEM((4, K, LY), f32),
            pltpu.VMEM((4, K, LY), f32),
            pltpu.VMEM((6, K, LY), f32),
            pltpu.VMEM((K * LX, LY), f32),
            pltpu.VMEM((K * LX, LY), f32),
            pltpu.VMEM((K * LX, LY), f32),
            pltpu.VMEM((NX, LY), f32),
            pltpu.VMEM((N, 136, LY), f32),
            pltpu.VMEM((N, 136, LY), f32),
            pltpu.VMEM((2, 2 * MSG, NY // 2 + LANES), bf16),
            pltpu.VMEM((3, NY, NY), bf16),
            pltpu.VMEM((N * 128, LANES), f32),
            pltpu.VMEM((N, 8, LANES), f32),
            pltpu.VMEM((S, 2, LANES), f32),
            pltpu.VMEM((S, 2, LANES), f32),
            pltpu.VMEM((S, 2, LANES), f32),
            pltpu.VMEM((S, 2, LANES), f32),
            pltpu.VMEM((2, S, LANES), f32),
            pltpu.VMEM((N * 128, LANES), f32),
            pltpu.VMEM((3 * MSG, NY), bf16),
            pltpu.VMEM((N, 136, LY), f32),
            pltpu.VMEM((N, 136, LY), f32),
            pltpu.VMEM((N, 8, LY), f32),
            pltpu.VMEM((N, 8, LY), f32),
            pltpu.VMEM((128, LANES), f32),
            pltpu.VMEM((NX, LY), f32),
            pltpu.VMEM((NX, LY), f32),
            pltpu.VMEM((NX, LY), f32),
            pltpu.VMEM((4, VIEWS, LY), f32),
            pltpu.VMEM((6 * VIEWS, 3 * LY), bf16),
            pltpu.VMEM((NX, 3 * LY), f32),
            pltpu.VMEM((NX, LY), f32),
            pltpu.VMEM((K * LX, LY), f32),
            dma((8,)), dma((8,)),
            dma((S,)), dma((S,)),
            dma((N,)), dma((N,)),
            dma((S,)), dma((S,)),
            dma((S,)), dma((S,)),
            dma((N,)), dma((N,)),
            dma((S,)), dma((S,)),
            dma((N,)), dma((N,)),
            dma((3,)),
        ]
        density_new, velocity_new, images, gradient = pl.pallas_call(
            functools.partial(step_kernel, (S, N, LX, K, VIEWS)),
            out_shape=(
                jax.ShapeDtypeStruct((LX * K, LY), f32),
                jax.ShapeDtypeStruct((3 * LX * K, LY), f32),
                jax.ShapeDtypeStruct(targets.shape, f32),
                jax.ShapeDtypeStruct((LX * K, LY), f32),
            ),
            in_specs=[anywhere] * 4 + [vmem, smem, smem, anywhere, vmem, vmem],
            out_specs=(anywhere, anywhere, vmem, anywhere),
            scratch_shapes=scratch,
            compiler_params=pltpu.CompilerParams(
                collective_id=0, has_side_effects=True, vmem_limit_bytes=60 * 1024 * 1024
            ),
        )(density, velocity, stencil_code, fractions, targets, view_start, view_sign, tables, lines, firsts)
        results = (density_new, velocity_new, images, gradient)
        shapes = tuple(jax.ShapeDtypeStruct(value.shape, value.dtype) for value in results)
        density_new, velocity_new, images, gradient = pl.pallas_call(
            hand_over,
            out_shape=shapes,
            in_specs=[anywhere] * 4,
            out_specs=(anywhere,) * 4,
            scratch_shapes=[pltpu.VMEM(shape.shape, f32) for shape in shapes] + [dma((32,)), dma((32,))],
            compiler_params=pltpu.CompilerParams(vmem_limit_bytes=60 * 1024 * 1024),
        )(*results)
        return (
            density_new.reshape(LX, K, LY),
            velocity_new.reshape(3, LX, K, LY),
            images,
            gradient.reshape(LX, K, LY),
        )

    return jax.shard_map(
        shards,
        mesh=mesh,
        in_specs=(
            P("sim", None, "pen"),
            P(None, "sim", None, "pen"),
            P("sim", None, "pen"),
            P(None, "sim", None, "pen"),
            P(None, "sim", "pen"),
            P(),
            P(),
        ),
        out_specs=(
            P("sim", None, "pen"),
            P(None, "sim", None, "pen"),
            P(None, "sim", "pen"),
            P("sim", None, "pen"),
        ),
        check_vma=False,
    )
```

```python
import functools

import jax
import jax.numpy as jnp
import numpy as np
from jax import lax
from jax.experimental import pallas as pl
from jax.experimental.pallas import tpu as pltpu
from jax.sharding import PartitionSpec as P

STEPS = 256
ABSORB = 2.0 / STEPS
LANES = 128
SEGMENTS = 8
MSG = 144
f32 = jnp.float32
bf16 = jnp.bfloat16


def hartley_pieces(length):
    index = np.arange(length)
    angles = (np.outer(index, index) % length) * (2.0 * np.pi / length)
    table = (np.cos(angles) + np.sin(angles)) / np.sqrt(length)
    pieces = []
    for _ in range(3):
        piece = table.astype(jnp.bfloat16)
        pieces.append(piece)
        table = table - piece.astype(np.float64)
    return np.stack(pieces)


def line_tables(length_y, length_x, local_x, layers):
    eig = 4.0 * np.sin(np.pi * np.arange(length_y) / length_y) ** 2
    half = eig / 2.0
    root = 1.0 / (1.0 + half + np.sqrt(half * (half + 2.0)))
    gap = 1.0 / root - root
    gap[0] = 1.0
    forward = -1.0 / gap
    backward = -1.0 / gap
    forward[0] = 1.0
    backward[0] = 0.0
    block = root**local_x
    closing = 1.0 - root**length_x
    closing[0] = 1.0
    closing = 1.0 / closing
    closing[0] = 0.0
    rows = np.stack([root, 1.0 / root, forward, backward, block, closing])
    rows = rows.reshape(6, length_y // LANES, 1, LANES)
    return np.repeat(rows, layers, axis=2).reshape(6, -1, LANES).astype(np.float32)


def split_two(values):
    high = values.astype(bf16)
    low = (values - high.astype(f32)).astype(bf16)
    return high, low


def split_three(values):
    high = values.astype(bf16)
    rest = values - high.astype(f32)
    mid = rest.astype(bf16)
    low = (rest - mid.astype(f32)).astype(bf16)
    return high, mid, low


def iota(shape, dim):
    return lax.broadcasted_iota(jnp.int32, shape, dim)


def matmul(a, b):
    return jnp.dot(a, b, preferred_element_type=f32)


def step_kernel(
    sizes,
    dens_hbm, vel_hbm, code_hbm, frac_hbm, targ, vstart, vsign, tables_hbm, lines, q_first,
    o_dens_hbm, o_vel_hbm, o_img, o_grad_hbm,
    dens, vel, code, frac, o_dens, o_vel, o_grad, io_sem,
    ext, pack, xlo, xhi, pin, dens_k, ax_k, ay_k,
    rays, d_send, d_in, x_pieces, q_tab, spec, spec_end,
    c_send, c_in, c_out, c_ret, ends, p_spec, y_pieces, o_send, o_in, h_send, h_in, h_columns,
    prefix, w_light, v_light, gathered, rhs, sums, g_send, g_in,
    halo_s, halo_r, dens_s, dens_r, d_s, d_r, c_s, c_r, b_s, b_r, o_s, o_r, g_s, g_r, h_s, h_r, tab_sem,
):
    S, N, LX, K, VIEWS = sizes
    KP = K // N
    NX, NY = S * LX, N * LANES
    ROWS = KP * LX
    SENT = ROWS + 8
    SEG = NX // SEGMENTS
    me = lax.axis_index("sim")
    pe = lax.axis_index("pen")

    def simp(off):
        return lax.rem(me + off + S, S)

    def penp(off):
        return lax.rem(pe + off + N, N)

    def balanced(i, count):
        odd = lax.rem(i, 2)
        half = (i + 1) // 2
        return odd * half + (1 - odd) * (count - half)

    parts = LX // 2
    fields_in = [pltpu.make_async_copy(dens_hbm.at[pl.ds(h * parts, parts)], dens.at[pl.ds(h * parts, parts)], io_sem.at[h]) for h in range(2)]
    fields_in += [
        pltpu.make_async_copy(vel_hbm.at[c, pl.ds(h * parts, parts)], vel.at[c, pl.ds(h * parts, parts)], io_sem.at[2 + 2 * c + h])
        for c in range(3)
        for h in range(2)
    ]
    weights_in = [pltpu.make_async_copy(code_hbm, code, io_sem.at[8])]
    weights_in += [pltpu.make_async_copy(frac_hbm.at[c], frac.at[c], io_sem.at[9 + c]) for c in range(3)]
    for copy in fields_in:
        copy.start()
    table_copies = [pltpu.make_async_copy(tables_hbm.at[t], q_tab.at[t], tab_sem.at[t]) for t in range(3)]

    barrier = pltpu.get_barrier_semaphore()

    def greet_sim(off, _):
        pl.semaphore_signal(barrier, inc=1, device_id={"sim": simp(off), "pen": pe}, device_id_type=pl.DeviceIdType.MESH)
        return 0

    def greet_pen(off, _):
        pl.semaphore_signal(barrier, inc=1, device_id={"sim": me, "pen": penp(off)}, device_id_type=pl.DeviceIdType.MESH)
        return 0

    lax.fori_loop(1, S, greet_sim, 0)
    lax.fori_loop(1, N, greet_pen, 0)
    corners = ((-1, -1), (-1, 1), (1, -1), (1, 1))
    for dx, dy in corners:
        pl.semaphore_signal(barrier, inc=1, device_id={"sim": simp(dx), "pen": penp(dy)}, device_id_type=pl.DeviceIdType.MESH)

    for copy in fields_in:
        copy.wait()
    for copy in weights_in:
        copy.start()

    lane = iota((K, LANES), 1)

    def source(field, x):
        return dens[x] if field == 0 else vel[field - 1, x]

    def pack_body(x, carry):
        first, last = carry
        for field in range(4):
            cells = source(field, x)
            spot = field * LX + x
            here = lane == spot
            first = jnp.where(here, pltpu.roll(cells, spot, 1), first)
            last = jnp.where(here, pltpu.roll(cells, lax.rem(spot + 1, LANES), 1), last)
        return first, last

    nothing = jnp.zeros((K, LANES), f32)
    first, last = lax.fori_loop(0, LX, pack_body, (nothing, nothing), unroll=16)
    pack[0] = first
    pack[1] = last
    for field in range(4):
        pack[2 + field] = source(field, 0)
        pack[6 + field] = source(field, LX - 1)

    pl.semaphore_wait(barrier, (S - 1) + (N - 1) + 4)

    def remote(src, dst, s_sem, r_sem, sim, pen):
        return pltpu.make_async_remote_copy(
            src_ref=src, dst_ref=dst, send_sem=s_sem, recv_sem=r_sem,
            device_id={"sim": sim, "pen": pen}, device_id_type=pl.DeviceIdType.MESH,
        )

    halo = [
        remote(pack.at[pl.ds(6, 4)], xlo, halo_s.at[0], halo_r.at[0], simp(1), pe),
        remote(pack.at[pl.ds(2, 4)], xhi, halo_s.at[1], halo_r.at[1], simp(-1), pe),
    ]
    for side in range(2):
        for dx in (-1, 0, 1):
            slot = side * 3 + 1 + dx
            halo.append(
                remote(
                    pack.at[1 - side], pin.at[slot], halo_s.at[2 + slot], halo_r.at[2 + slot],
                    simp(-dx), penp(1 if side == 0 else -1),
                )
            )
    for copy in halo:
        copy.start()
    for copy in table_copies:
        copy.start()

    def spread_body(x, _):
        for field in range(4):
            cells = source(field, x)
            ext[0, field, x + 1] = pltpu.roll(cells, 1, 1)
            ext[1, field, x + 1] = cells
            ext[2, field, x + 1] = pltpu.roll(cells, LANES - 1, 1)
        return 0

    lax.fori_loop(0, LX, spread_body, 0, unroll=4)
    for copy in halo:
        copy.wait()

    is_first = lane == 0
    is_last = lane == LANES - 1

    def fix_body(x, _):
        for field in range(4):
            spot = field * LX + x
            left = pltpu.roll(pin[1], LANES - spot, 1)
            right = pltpu.roll(pin[4], LANES - 1 - spot, 1)
            ext[0, field, x + 1] = jnp.where(is_first, left, ext[0, field, x + 1])
            ext[2, field, x + 1] = jnp.where(is_last, right, ext[2, field, x + 1])
        return 0

    lax.fori_loop(0, LX, fix_body, 0, unroll=16)
    for row, rows, slot, at in ((0, xlo, 0, LX - 1), (LX + 1, xhi, 2, 0)):
        for field in range(4):
            spot = field * LX + at
            cells = rows[field]
            left = pltpu.roll(pin[slot], (LANES - spot) % LANES, 1)
            right = pltpu.roll(pin[3 + slot], LANES - 1 - spot, 1)
            ext[0, field, row] = jnp.where(is_first, left, pltpu.roll(cells, 1, 1))
            ext[1, field, row] = cells
            ext[2, field, row] = jnp.where(is_last, right, pltpu.roll(cells, LANES - 1, 1))

    for copy in weights_in:
        copy.wait()

    def weights(bit, fraction):
        rest = 1.0 - fraction
        on = bit == 1
        return (jnp.where(on, rest, 0.0), jnp.where(on, fraction, rest), jnp.where(on, 0.0, fraction))

    def advect_body(x, _):
        codes = code[x]
        wx = weights(codes & 1, frac[0, x])
        wz = weights((codes >> 1) & 1, frac[1, x])
        wy = weights((codes >> 2) & 1, frac[2, x])
        totals = [None] * 4
        for slot, shift in ((1, 0), (0, -1), (2, 1)):
            if shift == 0:
                rx, ry = wx, wy
            else:
                amount = shift % K
                rx = [pltpu.roll(w, amount, 0) for w in wx]
                ry = [pltpu.roll(w, amount, 0) for w in wy]
            for field in range(4):
                term = None
                for sy in range(3):
                    part = (
                        rx[0] * ext[sy, field, x]
                        + rx[1] * ext[sy, field, x + 1]
                        + rx[2] * ext[sy, field, x + 2]
                    )
                    term = ry[sy] * part if term is None else term + ry[sy] * part
                if shift != 0:
                    term = pltpu.roll(term, (-shift) % K, 0)
                term = wz[slot] * term
                totals[field] = term if totals[field] is None else totals[field] + term
        o_dens[pl.ds(pl.multiple_of(x * K, 8), K), :] = totals[0]
        o_vel[pl.ds(pl.multiple_of(LX * K + x * K, 8), K), :] = totals[2]
        dens_k[pl.ds(x, K, stride=LX), :] = totals[0]
        ax_k[pl.ds(x, K, stride=LX), :] = totals[1]
        ay_k[pl.ds(x, K, stride=LX), :] = totals[3]
        return 0

    lax.fori_loop(0, LX, advect_body, 0, unroll=2)
    block = LX * K
    stores = [
        pltpu.make_async_copy(o_dens, o_dens_hbm, io_sem.at[12]),
        pltpu.make_async_copy(o_vel.at[pl.ds(block, block)], o_vel_hbm.at[pl.ds(block, block)], io_sem.at[13]),
    ]
    for copy in stores:
        copy.start()

    def sim_exchange(src, src_rows, dst, s_sem, r_sem):
        def descriptor(peer, start_at):
            if src_rows:
                a = src.at[pl.ds(pl.multiple_of(peer * src_rows, 8), src_rows)]
                b = dst.at[pl.ds(pl.multiple_of(start_at * src_rows, 8), src_rows)]
            else:
                a, b = src.at[peer], dst.at[start_at]
            return remote(a, b, s_sem.at[peer], r_sem.at[start_at], peer, pe)

        def start(first=1, end=S):
            def body(i, _):
                descriptor(simp(balanced(i, S)), me).start()
                return 0

            lax.fori_loop(first, end, body, 0, unroll=4)

        def wait_recv():
            def body(off, _):
                peer = simp(off)
                descriptor(peer, peer).wait_recv()
                return 0

            lax.fori_loop(1, S, body, 0)

        def wait_send():
            def body(off, _):
                descriptor(simp(off), me).wait_send()
                return 0

            lax.fori_loop(1, S, body, 0)

        def wait_one(i):
            peer = simp(balanced(i, S))
            descriptor(peer, peer).wait_recv()

        return start, wait_recv, wait_send, wait_one

    half = N // 2
    near_base = lax.div(pe, half) * half
    far_base = half - near_base

    def pen_peer(i):
        near = near_base + lax.rem(pe - near_base + 1 + i, half)
        return jnp.where(i < half, far_base + i, near)

    def pen_exchange(src, dst, s_sem, r_sem):
        def descriptor(peer, start_at):
            return remote(src.at[peer], dst.at[start_at], s_sem.at[peer], r_sem.at[start_at], me, peer)

        def loop(method, swap):
            def run(first=0, end=N - 1):
                def body(i, _):
                    peer = pen_peer(i)
                    getattr(descriptor(peer, peer if swap else pe), method)()
                    return 0

                lax.fori_loop(first, end, body, 0)

            return run

        return loop("start", False), loop("wait_recv", True), loop("wait_send", False)

    dens_x = sim_exchange(dens_k, LX, rays, dens_s, dens_r)
    early = S // 4
    dens_x[0](1, early)
    mine = pl.ds(pl.multiple_of(me * LX, 8), LX)
    rays[mine, :] = dens_k[mine, :]

    sub_x = iota((LX, LANES), 0)
    lane_x = iota((LX, LANES), 1)

    def div_part(part):
        base = part * ROWS
        ends = []
        for layer in range(KP):
            at = pl.ds(pl.multiple_of(base + layer * LX, 8), LX)
            ax = ax_k[at, :]
            ay = ay_k[at, :]
            before_x = jnp.where(sub_x == 0, 0.0, pltpu.roll(ax, 1, 0))
            before_y = jnp.where(lane_x == 0, 0.0, pltpu.roll(ay, 1, 1))
            d_send[part, layer * LX : (layer + 1) * LX, :] = (ax - before_x) + (ay - before_y)
            ends.append(-ax[LX - 1 : LX, :])
        turned = jnp.transpose(ay_k[pl.ds(pl.multiple_of(base, 8), ROWS), :])
        ends.append(turned[LANES - 1 : LANES, :])
        d_send[part, ROWS:SENT, :] = jnp.concatenate(ends + [jnp.zeros((7 - KP, LANES), f32)], axis=0)

    d_x = pen_exchange(d_send, d_in, d_s, d_r)

    def div_send(i, _):
        div_part(pen_peer(i))
        d_x[0](i, i + 1)
        return 0

    lax.fori_loop(0, N - 1, div_send, 0)
    div_part(pe)
    dens_x[0](early, S)
    d_in[pe] = d_send[pe]
    for copy in table_copies:
        copy.wait()

    WIDE = half * LANES

    def stage(group, at, cells, end):
        for t, piece in enumerate(split_two(cells)):
            x_pieces[group, t * MSG : t * MSG + ROWS, at] = piece
        for t, piece in enumerate(split_two(end)):
            x_pieces[group, t * MSG + ROWS : (t + 1) * MSG, at] = piece

    def stage_group(group, base):
        for j in range(half):
            cells = d_in[base + j, 0:ROWS, :]
            end = jnp.concatenate([d_in[base + j, ROWS : ROWS + KP, :], jnp.zeros((MSG - ROWS - KP, LANES), f32)], axis=0)
            stage(group, slice(j * LANES, (j + 1) * LANES), cells, end)

    def transform(group, table, rows, columns):
        wide = 2 * LANES

        def body(n, _):
            at = pl.ds(pl.multiple_of(n * wide, wide), wide)
            both = matmul(x_pieces[group, :, columns], table[0, rows, at])
            high = matmul(x_pieces[group, 0:MSG, columns], table[1, rows, at])
            result = both[0:MSG] + (both[MSG : 2 * MSG] + high)
            for side in range(2):
                values = result[:, side * LANES : (side + 1) * LANES]
                line = pl.ds(pl.multiple_of((2 * n + side) * ROWS, 8), ROWS)
                if group == 0:
                    spec[line, :] = values[0:ROWS]
                    spec_end[2 * n + side] = values[ROWS : ROWS + 8]
                else:
                    spec[line, :] = spec[line, :] + values[0:ROWS]
                    spec_end[2 * n + side] = spec_end[2 * n + side] + values[ROWS : ROWS + 8]
            return 0

        lax.fori_loop(0, NY // wide, body, 0)

    d_x[1](half, N - 1)
    stage_group(0, near_base)
    transform(0, q_tab, pl.ds(pl.multiple_of(near_base * LANES, LANES), WIDE), slice(0, WIDE))
    d_x[1](0, half)
    stage_group(1, far_base)
    ahead = jnp.concatenate(
        [d_in[part, ROWS + KP : ROWS + KP + 1, :] for part in range(N)] + [jnp.zeros((LANES - N, ROWS), f32)], axis=0
    )
    stage(1, slice(WIDE, WIDE + LANES), -jnp.transpose(ahead), jnp.zeros((MSG - ROWS, LANES), f32))
    transform(1, q_tab, pl.ds(pl.multiple_of(far_base * LANES, LANES), WIDE), slice(0, WIDE))
    transform(1, q_first, slice(0, LANES), slice(WIDE, WIDE + LANES))

    LINES = N * KP
    root = lines[0]
    root_inv = lines[1]
    beyond = jnp.concatenate([spec_end[part, 0:KP, :] for part in range(N)], axis=0)
    flat = jnp.zeros((LINES, LANES), f32)

    def at_x(x):
        return pl.ds(x, LINES, stride=LX)

    def ends_body(i, carry):
        fwd, bwd, acc = carry
        fwd = spec[at_x(i), :] + root * fwd
        acc = acc + fwd
        bwd = root * (spec[at_x(LX - 1 - i), :] + bwd)
        return fwd, bwd, acc

    fwd, bwd, acc = lax.fori_loop(0, LX, ends_body, (flat, root * beyond, flat), unroll=4)
    fwd = fwd + root_inv * beyond

    alone = jnp.logical_and(iota((LINES, LANES), 1) == 0, iota((LINES, LANES), 0) < KP)
    bwd = jnp.where(alone, acc, bwd)
    for line in range(LINES):
        c_send[line, 0:1, :] = fwd[line : line + 1]
        c_send[line, 1:2, :] = bwd[line : line + 1]
    c_x = sim_exchange(c_send, 0, c_in, c_s, c_r)
    c_x[0]()
    c_in[me] = c_send[me]

    dens_x[1]()

    def strided(x):
        return pl.ds(x, SEGMENTS, stride=SEG)

    def chain(x):
        return pl.ds(pl.multiple_of(x * SEGMENTS, SEGMENTS), SEGMENTS)

    seg0 = jnp.zeros((SEGMENTS, LANES), f32)

    def scan_body(i, carry):
        depth, down, up = carry
        back = SEG - 1 - i
        glow = ABSORB * rays[strided(i), :]
        prefix[chain(i), :] = depth
        depth = depth + glow
        down = glow + jnp.exp(-glow) * down
        v_light[chain(i), :] = down
        glow_b = ABSORB * rays[strided(back), :]
        up = glow_b + jnp.exp(-glow_b) * up
        w_light[chain(back), :] = up
        return depth, down, up

    seg_depth, seg_down, seg_up = lax.fori_loop(0, SEG, scan_body, (seg0, seg0, seg0), unroll=4)
    seg_pass = jnp.exp(-seg_depth)
    one = jnp.zeros((1, LANES), f32)
    total_depth, run_down, run_up = one, one, one
    starts = []
    for g in range(SEGMENTS):
        starts.append(total_depth)
        total_depth = total_depth + seg_depth[g : g + 1, :]
        run_down = seg_down[g : g + 1, :] + seg_pass[g : g + 1, :] * run_down
        h = SEGMENTS - 1 - g
        run_up = seg_up[h : h + 1, :] + seg_pass[h : h + 1, :] * run_up
    total_pass = jnp.exp(-total_depth)
    closing = 1.0 / (1.0 - total_pass)
    run_down = run_down * closing
    run_up = run_up * closing
    downs, ups = [], []
    for g in range(SEGMENTS):
        downs.append(run_down)
        run_down = seg_down[g : g + 1, :] + seg_pass[g : g + 1, :] * run_down
        h = SEGMENTS - 1 - g
        ups.append(run_up)
        run_up = seg_up[h : h + 1, :] + seg_pass[h : h + 1, :] * run_up
    start_depth = jnp.concatenate(starts, axis=0)
    down_in = jnp.concatenate(downs, axis=0)
    up_in = jnp.concatenate(ups[::-1], axis=0)

    def finish_body(i, _):
        glow = ABSORB * rays[strided(i), :]
        depth = prefix[chain(i), :]
        v_light[chain(i), :] = v_light[chain(i), :] + jnp.exp(-(depth + glow)) * down_in
        w_light[chain(i), :] = w_light[chain(i), :] + jnp.exp(depth - seg_depth) * up_in
        prefix[chain(i), :] = depth + start_depth
        return 0

    lax.fori_loop(0, SEG, finish_body, 0, unroll=4)

    c_x[1]()
    power = lines[4, pl.ds(me, 1), :]
    close = lines[5, pl.ds(me, 1), :]
    lone = jnp.logical_and(iota((1, LANES), 1) == 0, me < KP)

    def around_body(i, carry):
        a, b = carry
        a = c_in[i, 0:1, :] + power * a
        b = c_in[S - 1 - i, 1:2, :] + power * b
        return a, b

    a, b = lax.fori_loop(0, S, around_body, (one, one), unroll=8)

    def carry_body(i, carry):
        a, b, total = carry
        j = S - 1 - i
        c_out[i, 0:1, :] = a
        c_out[j, 1:2, :] = b
        total = total + (c_in[i, 1:2, :] + LX * a)
        return c_in[i, 0:1, :] + power * a, c_in[j, 1:2, :] + power * b, total

    _, _, total = lax.fori_loop(0, S, carry_body, (a * close, b * close, one), unroll=8)
    mean = total * (1.0 / NX)

    def lone_body(i, offset):
        slope = c_out[i, 0:1, :] - mean
        c_out[i, 0:1, :] = jnp.where(lone, slope, c_out[i, 0:1, :])
        c_out[i, 1:2, :] = jnp.where(lone, offset, c_out[i, 1:2, :])
        return offset + (c_in[i, 1:2, :] + LX * slope)

    lax.fori_loop(0, S, lone_body, one, unroll=8)
    b_x = sim_exchange(c_out, 0, c_ret, b_s, b_r)
    b_x[0]()
    c_ret[me] = c_out[me]

    sub_v = iota((VIEWS, LANES), 0)
    lane_m = iota((1, 6 * VIEWS), 1)
    view_m = lax.rem(lane_m, VIEWS)

    def where_is(x):
        return lax.rem(x, SEG) * SEGMENTS + lax.div(x, SEG)

    def view_body(v, carry):
        ups_v, start_m, up_m = carry
        x0 = vstart[v]
        up = vsign[v] == 1
        far = jnp.where(up, x0 + STEPS, x0 - STEPS)
        wraps = jnp.logical_or(far >= NX, far < 0)
        xe = jnp.where(far >= NX, far - NX, jnp.where(far < 0, far + NX, far))
        out = []
        for x in (x0, xe):
            at = pl.ds(where_is(x), 1)
            depth = prefix[at, :]
            depth = jnp.where(up, depth, -(depth + ABSORB * rays[pl.ds(x, 1), :]))
            out.append((depth, jnp.where(up, w_light[at, :], v_light[at, :])))
        gathered[0, pl.ds(v, 1), :] = out[0][0]
        gathered[1, pl.ds(v, 1), :] = out[0][1]
        gathered[2, pl.ds(v, 1), :] = out[1][0] + jnp.where(wraps, total_depth, 0.0)
        gathered[3, pl.ds(v, 1), :] = out[1][1]
        flag = vsign[v]
        return (
            jnp.where(sub_v == v, flag, ups_v),
            jnp.where(view_m == v, x0, start_m),
            jnp.where(view_m == v, flag, up_m),
        )

    none_m = jnp.zeros((1, 6 * VIEWS), jnp.int32)
    ups_v, start_m, up_m = lax.fori_loop(0, VIEWS, view_body, (jnp.zeros((VIEWS, LANES), jnp.int32), none_m, none_m))
    entry, light0, leave, light1 = gathered[0], gathered[1], gathered[2], gathered[3]
    seen_through = jnp.exp(entry - leave) * light1
    picture = light0 - seen_through
    o_img[:, 0, :] = picture
    pull = (STEPS * ABSORB) * (picture - targ[:, 0, :])
    coef = pull * jnp.exp(entry)
    alpha = jnp.where(ups_v == 1, coef, 0.0)
    gamma = jnp.where(ups_v == 1, 0.0, coef)
    beta = pull * seen_through
    for slot, value in enumerate((alpha, gamma, beta)):
        wrapped = beta if slot == 2 else value * total_pass
        both = jnp.concatenate([value, wrapped], axis=0)
        for t, piece in enumerate(split_three(both)):
            rhs[t * 2 * VIEWS : (t + 1) * 2 * VIEWS, slot * LANES : (slot + 1) * LANES] = piece

    kind = lax.rem(lax.div(lane_m, VIEWS), 2) == 1
    tile = 256

    def window_body(n, _):
        row = n * tile + iota((tile, 6 * VIEWS), 0)
        x = lax.rem(row, SEGMENTS) * SEG + lax.div(row, SEGMENTS)
        delta = jnp.where(up_m == 1, x - start_m, start_m - x)
        back = delta < 0
        inside = jnp.where(back, delta + NX, delta) < STEPS
        chosen = jnp.logical_and(inside, jnp.logical_xor(back, jnp.logical_not(kind)))
        mask = jnp.where(chosen, 1.0, 0.0).astype(bf16)
        sums[pl.ds(pl.multiple_of(n * tile, tile), tile), :] = matmul(mask, rhs[...])
        return 0

    lax.fori_loop(0, NX // tile, window_body, 0)

    def grad_body(i, _):
        glow = ABSORB * rays[strided(i), :]
        depth = prefix[chain(i), :]
        terms = sums[chain(i), :]
        g_send[strided(i), :] = (
            jnp.exp(-depth) * (1.0 - w_light[chain(i), :] + glow) * terms[:, 0:LANES]
            + jnp.exp(depth + glow) * (1.0 - v_light[chain(i), :] + glow) * terms[:, LANES : 2 * LANES]
            + terms[:, 2 * LANES : 3 * LANES]
        )
        return 0

    lax.fori_loop(0, SEG, grad_body, 0, unroll=4)
    g_x = sim_exchange(g_send, LX, g_in, g_s, g_r)
    g_x[0](1, S // 2)
    g_in[mine, :] = g_send[mine, :]

    b_x[1]()
    factor_f = lines[2]
    factor_b = lines[3]
    for line in range(LINES):
        ends[0, line : line + 1, :] = c_ret[line, 0:1, :]
        ends[1, line : line + 1, :] = c_ret[line, 1:2, :]
    first_f = ends[0]
    tail = ends[1]
    back_in = tail + root * beyond

    def back_body(i, bwd):
        x = LX - 1 - i
        p_spec[at_x(x), :] = factor_b * bwd
        return root * (spec[at_x(x), :] + bwd)

    lax.fori_loop(0, LX, back_body, back_in, unroll=4)

    def front_body(x, carry):
        fwd, height = carry
        fwd = spec[at_x(x), :] + root * fwd
        p_spec[at_x(x), :] = p_spec[at_x(x), :] + factor_f * jnp.where(alone, height, fwd)
        return fwd, height + fwd

    fwd, height = lax.fori_loop(0, LX, front_body, (first_f, tail), unroll=4)
    after = factor_f * jnp.where(alone, height, root * fwd) + factor_b * (root_inv * back_in)
    for part in range(N):
        at = slice(part * LANES, (part + 1) * LANES)
        for t, piece in enumerate(split_three(p_spec[part * ROWS : (part + 1) * ROWS, :])):
            y_pieces[t * MSG : t * MSG + ROWS, at] = piece
        end = jnp.concatenate([after[part * KP : (part + 1) * KP], jnp.zeros((MSG - ROWS - KP, LANES), f32)], axis=0)
        for t, piece in enumerate(split_three(end)):
            y_pieces[t * MSG + ROWS : (t + 1) * MSG, at] = piece

    def inverse(base, far):
        def body(n, _):
            wide = PAIR * LANES
            at = pl.ds(pl.multiple_of(base * LANES + n * wide, LANES), wide)
            first = matmul(y_pieces[...], q_tab[0, :, at])
            second = matmul(y_pieces[0 : 2 * MSG], q_tab[1, :, at])
            third = matmul(y_pieces[0:MSG], q_tab[2, :, at])
            small = second[MSG : 2 * MSG] + third + first[2 * MSG : 3 * MSG]
            result = first[0:MSG] + (first[MSG : 2 * MSG] + second[0:MSG] + small)
            for side in range(PAIR):
                o_send[base + PAIR * n + side] = result[0:SENT, side * LANES : (side + 1) * LANES]
            if far:
                o_x[0](PAIR * n, PAIR * (n + 1))
            return 0

        lax.fori_loop(0, half // PAIR, body, 0)

    PAIR = min(2, half)
    o_x = pen_exchange(o_send, o_in, o_s, o_r)
    inverse(far_base, True)
    inverse(near_base, False)
    o_x[0](half, N - 1)
    for part in range(N):
        turned = jnp.transpose(o_send[(part + 1) % N, 0:ROWS, :])
        h_send[part] = jnp.broadcast_to(turned[0:1, :], (8, ROWS))
    h_x = pen_exchange(h_send, h_in, h_s, h_r)
    h_x[0]()
    g_x[0](S // 2, S)
    o_in[pe] = o_send[pe]
    h_in[pe] = h_send[pe]

    def velocity_part(part):
        column = pltpu.roll(h_columns[...], LANES - 1 - part, 1)
        for layer in range(KP):
            k = part * KP + layer
            at = pl.ds(pl.multiple_of(k * LX, 8), LX)
            here = o_in[part, layer * LX : (layer + 1) * LX, :]
            above = o_in[part, ROWS + layer : ROWS + layer + 1, :]
            next_x = jnp.where(sub_x == LX - 1, above, pltpu.roll(here, LX - 1, 0))
            next_y = jnp.where(
                lane_x == LANES - 1, column[layer * LX : (layer + 1) * LX, :], pltpu.roll(here, LANES - 1, 1)
            )
            o_vel[pl.ds(k, LX, stride=K), :] = ax_k[at, :] - (next_x - here)
            o_vel[pl.ds(2 * LX * K + k, LX, stride=K), :] = ay_k[at, :] - (next_y - here)

    def velocity_group(base):
        def body(j, _):
            velocity_part(base + j)
            return 0

        lax.fori_loop(0, half, body, 0)

    h_x[1]()
    heads = jnp.concatenate([h_in[part, 0:1, :] for part in range(N)] + [jnp.zeros((LANES - N, ROWS), f32)], axis=0)
    h_columns[...] = jnp.transpose(heads)
    o_x[1](half, N - 1)
    velocity_group(near_base)

    def back_home(k):
        o_grad[pl.ds(k, LX, stride=K), :] = g_in[pl.ds(pl.multiple_of(k * LX, 8), LX), :]

    def bring_home(i, _):
        g_x[3](i)
        back_home(simp(balanced(i, S)))
        return 0

    back_home(me)
    lax.fori_loop(1, S // 2, bring_home, 0)

    def far_velocity(i, _):
        o_x[1](i, i + 1)
        velocity_part(far_base + i)
        return 0

    lax.fori_loop(0, half, far_velocity, 0)

    late = [
        pltpu.make_async_copy(o_vel.at[pl.ds(at, block // 2)], o_vel_hbm.at[pl.ds(at, block // 2)], io_sem.at[slot])
        for slot, at in ((14, 0), (15, block // 2), (16, 2 * block), (17, 2 * block + block // 2))
    ]
    for copy in late:
        copy.start()
    lax.fori_loop(S // 2, S, bring_home, 0)
    late += [
        pltpu.make_async_copy(o_grad.at[pl.ds(at, block // 2)], o_grad_hbm.at[pl.ds(at, block // 2)], io_sem.at[slot])
        for slot, at in ((18, 0), (19, block // 2))
    ]
    for copy in late[4:]:
        copy.start()
    for copy in stores + late:
        copy.wait()
    for copy_sends in (dens_x[2], d_x[2], c_x[2], b_x[2], g_x[2], o_x[2], h_x[2]):
        copy_sends()


def hand_over(*refs):
    count = (len(refs) - 2) // 3
    sources, targets, rooms = refs[:count], refs[count : 2 * count], refs[2 * count : 3 * count]
    in_sem, out_sem = refs[3 * count :]
    blocks = []
    for source, target, room in zip(sources, targets, rooms):
        rows = source.shape[0]
        size = min(rows, 512)
        for at in range(0, rows, size):
            part = pl.ds(at, size)
            slot = len(blocks)
            blocks.append(
                (
                    pltpu.make_async_copy(source.at[part], room.at[part], in_sem.at[slot]),
                    pltpu.make_async_copy(room.at[part], target.at[part], out_sem.at[slot]),
                )
            )
    for fetch, _ in blocks:
        fetch.start()
    for fetch, store in blocks:
        fetch.wait()
        store.start()
    for _, store in blocks:
        store.wait()


def solution(mesh):
    S, N = mesh.shape["sim"], mesh.shape["pen"]

    def shards(density, velocity, stencil_code, fractions, targets, view_start, view_sign):
        LX, K, LY = density.shape
        VIEWS = targets.shape[0]
        NX, NY = LX * S, LY * N
        pieces = hartley_pieces(NY)
        tables = jnp.asarray(pieces)
        chosen = pieces[0:2, (np.arange(1, N + 1) * LY) % NY]
        firsts = jnp.asarray(np.concatenate([chosen, np.zeros((2, LANES - N, NY), chosen.dtype)], axis=1))
        lines = jnp.asarray(line_tables(NY, NX, LX, K // N))
        anywhere = pl.BlockSpec(memory_space=pl.ANY)
        vmem = pl.BlockSpec(memory_space=pltpu.VMEM)
        smem = pl.BlockSpec(memory_space=pltpu.SMEM)
        dma = pltpu.SemaphoreType.DMA
        scratch = [
            pltpu.VMEM((LX, K, LY), f32),
            pltpu.VMEM((3, LX, K, LY), f32),
            pltpu.VMEM((LX, K, LY), jnp.int32),
            pltpu.VMEM((3, LX, K, LY), f32),
            pltpu.VMEM((LX * K, LY), f32),
            pltpu.VMEM((3 * LX * K, LY), f32),
            pltpu.VMEM((LX * K, LY), f32),
            dma((20,)),
            pltpu.VMEM((3, 4, LX + 2, K, LY), f32),
            pltpu.VMEM((10, K, LY), f32),
            pltpu.VMEM((4, K, LY), f32),
            pltpu.VMEM((4, K, LY), f32),
            pltpu.VMEM((6, K, LY), f32),
            pltpu.VMEM((K * LX, LY), f32),
            pltpu.VMEM((K * LX, LY), f32),
            pltpu.VMEM((K * LX, LY), f32),
            pltpu.VMEM((NX, LY), f32),
            pltpu.VMEM((N, 136, LY), f32),
            pltpu.VMEM((N, 136, LY), f32),
            pltpu.VMEM((2, 2 * MSG, NY // 2 + LANES), bf16),
            pltpu.VMEM((3, NY, NY), bf16),
            pltpu.VMEM((N * 128, LANES), f32),
            pltpu.VMEM((N, 8, LANES), f32),
            pltpu.VMEM((S, 2, LANES), f32),
            pltpu.VMEM((S, 2, LANES), f32),
            pltpu.VMEM((S, 2, LANES), f32),
            pltpu.VMEM((S, 2, LANES), f32),
            pltpu.VMEM((2, S, LANES), f32),
            pltpu.VMEM((N * 128, LANES), f32),
            pltpu.VMEM((3 * MSG, NY), bf16),
            pltpu.VMEM((N, 136, LY), f32),
            pltpu.VMEM((N, 136, LY), f32),
            pltpu.VMEM((N, 8, LY), f32),
            pltpu.VMEM((N, 8, LY), f32),
            pltpu.VMEM((128, LANES), f32),
            pltpu.VMEM((NX, LY), f32),
            pltpu.VMEM((NX, LY), f32),
            pltpu.VMEM((NX, LY), f32),
            pltpu.VMEM((4, VIEWS, LY), f32),
            pltpu.VMEM((6 * VIEWS, 3 * LY), bf16),
            pltpu.VMEM((NX, 3 * LY), f32),
            pltpu.VMEM((NX, LY), f32),
            pltpu.VMEM((K * LX, LY), f32),
            dma((8,)), dma((8,)),
            dma((S,)), dma((S,)),
            dma((N,)), dma((N,)),
            dma((S,)), dma((S,)),
            dma((S,)), dma((S,)),
            dma((N,)), dma((N,)),
            dma((S,)), dma((S,)),
            dma((N,)), dma((N,)),
            dma((3,)),
        ]
        density_new, velocity_new, images, gradient = pl.pallas_call(
            functools.partial(step_kernel, (S, N, LX, K, VIEWS)),
            out_shape=(
                jax.ShapeDtypeStruct((LX * K, LY), f32),
                jax.ShapeDtypeStruct((3 * LX * K, LY), f32),
                jax.ShapeDtypeStruct(targets.shape, f32),
                jax.ShapeDtypeStruct((LX * K, LY), f32),
            ),
            in_specs=[anywhere] * 4 + [vmem, smem, smem, anywhere, vmem, vmem],
            out_specs=(anywhere, anywhere, vmem, anywhere),
            scratch_shapes=scratch,
            compiler_params=pltpu.CompilerParams(
                collective_id=0, has_side_effects=True, vmem_limit_bytes=60 * 1024 * 1024
            ),
        )(density, velocity, stencil_code, fractions, targets, view_start, view_sign, tables, lines, firsts)
        results = (density_new, velocity_new, images, gradient)
        shapes = tuple(jax.ShapeDtypeStruct(value.shape, value.dtype) for value in results)
        density_new, velocity_new, images, gradient = pl.pallas_call(
            hand_over,
            out_shape=shapes,
            in_specs=[anywhere] * 4,
            out_specs=(anywhere,) * 4,
            scratch_shapes=[pltpu.VMEM(shape.shape, f32) for shape in shapes] + [dma((32,)), dma((32,))],
            compiler_params=pltpu.CompilerParams(vmem_limit_bytes=60 * 1024 * 1024),
        )(*results)
        return (
            density_new.reshape(LX, K, LY),
            velocity_new.reshape(3, LX, K, LY),
            images,
            gradient.reshape(LX, K, LY),
        )

    return jax.shard_map(
        shards,
        mesh=mesh,
        in_specs=(
            P("sim", None, "pen"),
            P(None, "sim", None, "pen"),
            P("sim", None, "pen"),
            P(None, "sim", None, "pen"),
            P(None, "sim", "pen"),
            P(),
            P(),
        ),
        out_specs=(
            P("sim", None, "pen"),
            P(None, "sim", None, "pen"),
            P(None, "sim", "pen"),
            P("sim", None, "pen"),
        ),
        check_vma=False,
    )
```
